32 devices in a mesh: bl: 8 (over z, y), comp: 4 (over x, core).
Axes of the slice: x: 2, y: 2, z: 4, core: 2. Of those that a mesh axis runs over, the one named last changes fastest.
Arguments:
- baseline_uvw: float32 [3, 8192], P(None, ('bl', 'comp')), may hold values from -96 to 96
- antenna_pair: int32 [2, 8192], P(None, ('bl', 'comp')), may hold values from 0 to 511, as said below
- row_count: int32 [32], P(('bl', 'comp')), may hold values from 32 to 256, as said below
- comp_position: float32 [2, 8192], P(None, 'comp'), may hold values from -0.3 to 0.3
- comp_flux: float32 [4, 16, 8192], P(None, None, 'comp'), may hold values from -0.0625 to 0.0625
- gain: float32 [512, 256], P(('bl', 'comp')), may hold values from -4.2 to 4.2
- antenna_owner: int32 [512], replicated, may hold values from 0 to 31, as said below
- observed: float32 [8192, 128], P(('bl', 'comp')), may hold values from -6 to 6
Outputs:
- residual: float32 [8192, 128], P(('bl', 'comp'))
- normal_blocks: float32 [512, 384], P(('bl', 'comp'))
The draws below stay inside these ranges and needn't reach their ends.
Inputs may be any that keep to these rules, and one draw needn't show every extreme that they name: `antenna_pair`: the two antennas of a row differ. `row_count`: a multiple of 32; slots at or beyond it on that device are padding; some device is full. `antenna_owner`: each of the 32 owners holds exactly 16 antennas.
All inputs are finite; a program needn't handle non-finite values.
Results may differ from the reference program's by a relative error of at most 0.0003.
Values sent between devices are 32-bit elements; how exact they have to be, the bound alone decides.
No kernel may reach another device: no remote copies, remote signals or barrier semaphores. Data moves between devices by JAX's collectives and lax.ppermute only.
A program may use at most 448 MiB of HBM per device.

```python
import math
import jax
import jax.numpy as jnp
from jax import lax

ANTENNAS = 512
CHANNELS = 16
TIMES = 4
ROW_DEV = 256
OWNERS = 32
A_DEV = 16
ROWS = 8192
COMPS = 8192


def draw_antenna_pair(key, part):
    first_key = jax.random.fold_in(key, 11)
    step_key = jax.random.fold_in(key, 12)
    first = jax.random.randint(first_key, (ROWS,), 0, ANTENNAS)
    offset = jax.random.randint(step_key, (ROWS,), 1, ANTENNAS)
    return jnp.stack([first, (first + offset) % ANTENNAS]).astype(jnp.int32)


def draw_row_count(key, part):
    level_key = jax.random.fold_in(key, 21)
    full_key = jax.random.fold_in(key, 22)
    eighths = jax.random.randint(level_key, (OWNERS,), 1, 9)
    chosen = jax.random.randint(full_key, (), 0, OWNERS)
    eighths = jnp.where(jnp.arange(OWNERS) == chosen, 8, eighths)
    return (eighths * (ROW_DEV // 8)).astype(jnp.int32)


def draw_antenna_owner(key, part):
    order = jax.random.permutation(jax.random.fold_in(key, 31), ANTENNAS)
    owners = (jnp.arange(ANTENNAS) // A_DEV).astype(jnp.int32)
    return jnp.zeros((ANTENNAS,), jnp.int32).at[order].set(owners)


def level_of(key, dims, split, smallest, largest):
    def one(axis_at, shards_of):
        heights = jax.random.uniform(jax.random.fold_in(jax.random.fold_in(key, 6), axis_at), (shards_of,), jnp.float32, smallest / len(split), largest / len(split))
        return jnp.repeat(jnp.exp(heights), dims[axis_at] // shards_of).reshape((-1,) + (1,) * (len(dims) - axis_at - 1))

    level = one(*split[0])
    for cut in split[1:]:
        level = level * one(*cut)
    return level


def scatter_about(rng, extent, scale, bound, shards=(), kind=jnp.bfloat16):
    array = scale * jax.random.normal(rng, extent, jnp.float32)
    if shards:
        array = array * level_of(rng, extent, shards, -0.22, 0.18)
    return jnp.clip(array, -bound, bound).astype(kind)


def setup_inputs(seed: int = 0) -> dict:
    key_of = jax.random.split(jax.random.key(seed), 9)
    return {
        "baseline_uvw": scatter_about(key_of[0], (3, ROWS), 16.0, 96.0, ((1, 32),), jnp.float32),
        "antenna_pair": draw_antenna_pair(jax.random.fold_in(key_of[8], 71), 0),
        "row_count": draw_row_count(jax.random.fold_in(key_of[8], 71), 0),
        "comp_position": jnp.clip(jax.random.uniform(key_of[3], (2, COMPS), jnp.float32, -0.3, 0.3) * level_of(key_of[3], (2, COMPS), ((1, 4),), -0.4, 0.0), -0.3, 0.3),
        "comp_flux": scatter_about(key_of[4], (4, CHANNELS, COMPS), COMPS ** -0.5, 0.0625, ((2, 4),), jnp.float32),
        "gain": scatter_about(key_of[5], (ANTENNAS, 4 * TIMES * CHANNELS), 0.7, 4.2, ((0, 32),), jnp.float32),
        "antenna_owner": draw_antenna_owner(jax.random.fold_in(key_of[8], 71), 0),
        "observed": scatter_about(key_of[7], (ROWS, 8 * CHANNELS), 1.0, 6.0, ((0, 32),), jnp.float32),
    }


HIGHEST = lax.Precision.HIGHEST
TWO_PI = 2.0 * math.pi

def predict(uvw, sky):
    count_rows = uvw.shape[1]
    count_comps = sky.shape[1]
    l_coord = sky[0]
    m_coord = sky[1]
    n_minus = jnp.sqrt(1.0 - l_coord * l_coord - m_coord * m_coord) - 1.0
    directions = jnp.stack([l_coord, m_coord, n_minus])
    base_phase = TWO_PI * jnp.dot(uvw.T, directions, precision=HIGHEST)
    flux = sky[2:].reshape(4, CHANNELS, count_comps)
    stokes_i = flux[0]
    stokes_q = flux[1]
    stokes_u = flux[2]
    stokes_v = flux[3]
    zeroes = jnp.zeros_like(stokes_i)
    bright_real = jnp.stack([stokes_i + stokes_q, stokes_u, stokes_u, stokes_i - stokes_q])
    bright_imag = jnp.stack([zeroes, stokes_v, -stokes_v, zeroes])
    columns = []
    for channel in range(CHANNELS):
        ratio = 1.0 + channel / (2.0 * CHANNELS)
        angle = base_phase * ratio
        waves = jnp.concatenate([jnp.cos(angle), jnp.sin(angle)], axis=1)
        upper = jnp.concatenate([bright_real[:, channel].T, bright_imag[:, channel].T], axis=1)
        lower = jnp.concatenate([bright_imag[:, channel].T, -bright_real[:, channel].T], axis=1)
        table = jnp.concatenate([upper, lower], axis=0)
        columns.append(jnp.dot(waves, table, precision=HIGHEST))
    return jnp.stack(columns, axis=2).reshape(count_rows, 8 * CHANNELS)

def owner_slots(antenna_owner, per_owner):
    count = antenna_owner.shape[0]
    index = jnp.arange(count, dtype=jnp.int32)
    same = (antenna_owner[None, :] == antenna_owner[:, None]) & (index[None, :] < index[:, None])
    rank = lax.optimization_barrier(jnp.sum(same.astype(jnp.int32), axis=1)).astype(jnp.int32)
    return (antenna_owner * per_owner + rank).astype(jnp.int32)

def row_slots(antennas, slots):
    index = jnp.arange(slots.shape[0], dtype=jnp.int32)
    picked = jnp.where(antennas[:, None] == index[None, :], slots[None, :], 0)
    return lax.optimization_barrier(jnp.sum(picked, axis=1)).astype(jnp.int32)

def calibrate(visibility, observed, gain_near, gain_far, live_count):
    rows = visibility.shape[0]
    slot_index = jnp.arange(rows, dtype=jnp.int32)
    live = (slot_index < live_count).astype(jnp.float32)
    time_index = slot_index % TIMES
    time_hot = (time_index[:, None] == jnp.arange(TIMES, dtype=jnp.int32)[None, :]).astype(jnp.float32)

    def pick(table):
        shaped = table.reshape(rows, TIMES, 2, 2, CHANNELS)
        return lax.optimization_barrier(jnp.sum(shaped * time_hot[:, :, None, None, None], axis=1))
    near_gain = pick(gain_near)
    far_gain = pick(gain_far)
    near_real = near_gain[:, 0][:, :, None, :]
    near_imag = near_gain[:, 1][:, :, None, :]
    far_real = far_gain[:, 0][:, None, :, :]
    far_imag = far_gain[:, 1][:, None, :, :]
    shaped_vis = visibility.reshape(rows, 2, 2, 2, CHANNELS)
    vis_real = shaped_vis[:, 0]
    vis_imag = shaped_vis[:, 1]
    shaped_obs = observed.reshape(rows, 2, 2, 2, CHANNELS)
    both_real = near_real * far_real + near_imag * far_imag
    both_imag = near_imag * far_real - near_real * far_imag
    model_real = both_real * vis_real - both_imag * vis_imag
    model_imag = both_real * vis_imag + both_imag * vis_real
    weight = live[:, None, None, None]
    res_real = weight * (shaped_obs[:, 0] - model_real)
    res_imag = weight * (shaped_obs[:, 1] - model_imag)
    near_zr = far_real * vis_real + far_imag * vis_imag
    near_zi = far_real * vis_imag - far_imag * vis_real
    near_terms = jnp.stack([lax.optimization_barrier(jnp.sum(weight * (near_zr * near_zr + near_zi * near_zi), axis=2)), lax.optimization_barrier(jnp.sum(near_zr * res_real + near_zi * res_imag, axis=2)), lax.optimization_barrier(jnp.sum(near_zr * res_imag - near_zi * res_real, axis=2))], axis=1)
    far_yr = near_real * vis_real - near_imag * vis_imag
    far_yi = near_real * vis_imag + near_imag * vis_real
    far_terms = jnp.stack([lax.optimization_barrier(jnp.sum(weight * (far_yr * far_yr + far_yi * far_yi), axis=1)), lax.optimization_barrier(jnp.sum(far_yr * res_real + far_yi * res_imag, axis=1)), lax.optimization_barrier(jnp.sum(far_yi * res_real - far_yr * res_imag, axis=1))], axis=1)
    spread = time_hot[:, :, None]
    near_terms = (spread * near_terms.reshape(rows, 1, 6 * CHANNELS)).reshape(rows, 6 * TIMES * CHANNELS)
    far_terms = (spread * far_terms.reshape(rows, 1, 6 * CHANNELS)).reshape(rows, 6 * TIMES * CHANNELS)
    residual = jnp.stack([res_real, res_imag], axis=1).reshape(rows, 8 * CHANNELS)
    return (residual, near_terms, far_terms)

def reference(baseline_uvw, antenna_pair, row_count, comp_position, comp_flux, gain, antenna_owner, observed):
    sky = jnp.concatenate([comp_position, comp_flux.reshape(4 * CHANNELS, COMPS)], axis=0)
    slots = owner_slots(antenna_owner, ANTENNAS // OWNERS)
    uvw_blocks = baseline_uvw.reshape(3, OWNERS, ROW_DEV).transpose(1, 0, 2)
    pair_blocks = antenna_pair.reshape(2, OWNERS, ROW_DEV).transpose(1, 0, 2)
    obs_blocks = observed.reshape(OWNERS, ROW_DEV, 8 * CHANNELS)
    columns = jnp.arange(ANTENNAS, dtype=jnp.int32)

    def one_block(total, items):
        uvw, pairs, live_count, obs = items
        visibility = predict(uvw, sky)
        slot_near = row_slots(pairs[0], slots)
        slot_far = row_slots(pairs[1], slots)
        hot_near = (slot_near[:, None] == columns[None, :]).astype(jnp.float32)
        hot_far = (slot_far[:, None] == columns[None, :]).astype(jnp.float32)
        gain_near = jnp.dot(hot_near, gain, precision=HIGHEST)
        gain_far = jnp.dot(hot_far, gain, precision=HIGHEST)
        residual, near_terms, far_terms = calibrate(visibility, obs, gain_near, gain_far, live_count)
        total = total + jnp.dot(hot_near.T, near_terms, precision=HIGHEST) + jnp.dot(hot_far.T, far_terms, precision=HIGHEST)
        return (total, residual)
    start = jnp.zeros((ANTENNAS, 6 * TIMES * CHANNELS), jnp.float32)
    normal, residuals = lax.scan(one_block, start, (uvw_blocks, pair_blocks, row_count, obs_blocks))
    return (residuals.reshape(ROWS, 8 * CHANNELS), normal)
```

```python
import jax
import jax.numpy as jnp
from jax import lax
from jax.experimental import pallas as pl
from jax.experimental.pallas import tpu as pltpu
from jax.sharding import PartitionSpec as P

CHANNELS = 16
TIMES = 4
GROUP = 4
LANES = 256
DEPTH = 256
STRIP = 16
F32 = jnp.float32
BF16 = jnp.bfloat16

SIN = [4 * v for v in (4.4428679030304945, -7.307443421264523, 3.5947880783696866, -0.7843740306721513)]
COS = [4 * v for v in (1.4142040804669556, -6.977642056688728, 5.71523839383031, -1.7283486597599615)]
CENTRES = (1 + 3.5 / 32, 1 + 11.5 / 32)
HALF_STEP = 1 / 64
TERMS = ((0, 0), (0, 1), (0, 2), (1, 0), (1, 1), (2, 0))


def pieces(x, count):
    out = []
    for _ in range(count):
        piece = lax.reduce_precision(x, 8, 7)
        out.append(piece.astype(BF16))
        x = x - piece
    return out


def turn(x):
    r = x - jnp.round(x)
    q = r * r
    s = (((SIN[3] * q + SIN[2]) * q + SIN[1]) * q + SIN[0]) * r
    c = ((COS[3] * q + COS[2]) * q + COS[1]) * q + COS[0]
    return 16.0 - s * s, s * c


def factors(t):
    out = []
    for centre in CENTRES:
        for v in turn(t * centre):
            hi = jnp.round(v)
            out += [hi.astype(BF16), (v - hi).astype(BF16)]
    c, s = turn(t * HALF_STEP)
    twice = (c * c) * (4.0 / 256.0) - 2.0
    cs, ss = [c, (twice - 1.0) * c], [s, (twice + 1.0) * s]
    for _ in range(2):
        cs.append(twice * cs[-1] - cs[-2])
        ss.append(twice * ss[-1] - ss[-2])
    for pair in zip(cs, ss):
        for v in pair:
            hi = jnp.round(v)
            out += [hi.astype(BF16), (v - hi).astype(BF16), v.astype(BF16)]
    return out


FACTORS = 32


def predict_kernel(blocks, n_ref, u_ref, l_ref, tab_ref, o_ref, fa, fb, tt, ta, tb, acc):
    total = ((n_ref[0] + LANES - 1) // LANES) * blocks

    def begin(index, table):
        index = jnp.minimum(index, total - 1)
        row, block = lax.div(index, blocks), lax.rem(index, blocks)
        comps = pl.ds(pl.multiple_of(block * DEPTH, DEPTH), DEPTH)
        tt[...] = jnp.dot(l_ref[comps, :], u_ref[row], preferred_element_type=F32)
        table[...] = tab_ref[block]

    def strip(j, f):
        rows = slice(j * STRIP, (j + 1) * STRIP)
        for i, v in enumerate(factors(tt[rows])):
            f[i, rows] = v

    def product(d, f, table):
        pair, which = d // 4, d % 4
        a, k = pair // 4, pair % 4
        x = 4 * a + (2 if which in (1, 2) else 0)
        y = 8 + 6 * k + (3 if which in (1, 3) else 0)
        hi = f[x] * f[y]
        lo = f[x + 1] * f[y + 2] + f[x] * f[y + 1]
        t = table[pair]
        acc[pair, which] += jnp.dot(t, hi, preferred_element_type=F32) + jnp.dot(
            t, lo, preferred_element_type=F32
        )

    strips = DEPTH // STRIP

    def step(f, g, table):
        done = 0
        for d in range(32):
            product(d, f, table)
            while done < (d + 1) * strips // 32:
                strip(done, g)
                done += 1

    def flush(row):
        sign = jnp.where(lax.broadcasted_iota(jnp.int32, (8, LANES), 0) < 4, -1.0, 1.0)
        for pair in range(8):
            a, k = pair // 4, pair % 4
            p = [(acc[pair, w, 0:8] + acc[pair, w, 8:16]) * (1.0 / 256.0) for w in range(4)]
            c = p[0] + sign * p[1]
            s = p[2] - sign * p[3]
            o_ref[2 * a + 1, row, k] = jnp.concatenate([c[0:4], s[0:4]], axis=0)
            o_ref[2 * a, row, 3 - k] = jnp.concatenate([c[4:8], s[4:8]], axis=0)
        acc[...] = jnp.zeros_like(acc)

    o_ref[...] = jnp.zeros_like(o_ref)
    acc[...] = jnp.zeros_like(acc)
    begin(0, ta)
    for j in range(strips):
        strip(j, fa)

    def body(i, carry):
        begin(2 * i + 1, tb)
        step(fa, fb, ta)
        begin(2 * i + 2, ta)
        step(fb, fa, tb)

        @pl.when(lax.rem(2 * i + 2, blocks) == 0)
        def _():
            flush(lax.div(2 * i, blocks))

        return carry

    lax.fori_loop(0, total // 2, body, 0)


def predict(live, uvw, position, flux):
    rows, comps = uvw.shape[1], position.shape[1]
    row_blocks, blocks = rows // LANES, comps // DEPTH
    l_coord, m_coord = position[0], position[1]
    n_minus = jnp.sqrt(1.0 - l_coord * l_coord - m_coord * m_coord) - 1.0
    up, lp = pieces(uvw, 3), pieces(jnp.stack([l_coord, m_coord, n_minus]), 3)
    pad = ((0, 32 - 3 * len(TERMS)), (0, 0))
    u = jnp.pad(jnp.concatenate([up[i] for i, _ in TERMS]), pad)
    l = jnp.pad(jnp.concatenate([lp[j] for _, j in TERMS]), pad)
    u = u.reshape(32, row_blocks, LANES).transpose(1, 0, 2)
    i, q, v, w = flux
    bright = jnp.stack([i + q, v, w, i - q], 1).reshape(2, 8, 4, comps)
    plus, minus = bright[:, 4:].reshape(8, 4, comps), bright[:, 3::-1].reshape(8, 4, comps)
    hi, lo = pieces(jnp.concatenate([plus, minus], 1), 2)
    table = jnp.concatenate([hi, lo], 1).reshape(8, 16, blocks, DEPTH).transpose(2, 0, 1, 3)
    vmem = pl.BlockSpec(memory_space=pltpu.VMEM)
    return pl.pallas_call(
        lambda *refs: predict_kernel(blocks, *refs),
        out_shape=jax.ShapeDtypeStruct((GROUP, row_blocks, 4, 8, LANES), F32),
        in_specs=[pl.BlockSpec(memory_space=pltpu.SMEM), vmem, vmem, vmem],
        out_specs=vmem,
        scratch_shapes=[
            pltpu.VMEM((FACTORS, DEPTH, LANES), BF16),
            pltpu.VMEM((FACTORS, DEPTH, LANES), BF16),
            pltpu.VMEM((DEPTH, LANES), F32),
            pltpu.VMEM((8, 16, DEPTH), BF16),
            pltpu.VMEM((8, 16, DEPTH), BF16),
            pltpu.VMEM((8, 4, 16, LANES), F32),
        ],
        compiler_params=pltpu.CompilerParams(vmem_limit_bytes=40 << 20),
        cost_estimate=pl.CostEstimate(
            flops=64 * 16 * rows * comps, bytes_accessed=4 << 20, transcendentals=0
        ),
        name="predict",
    )(live, u, l.T, table)


def calibrate_kernel(n_ref, slot_ref, vis_ref, obs_ref, gain_ref, res_ref, norm_ref):
    row_blocks, slots = vis_ref.shape[0], norm_ref.shape[0]
    norm_ref[...] = jnp.zeros_like(norm_ref)
    res_ref[...] = jnp.zeros_like(res_ref)

    def block(row, carry):
        lane = lax.broadcasted_iota(jnp.int32, (1, LANES), 1)
        weight = (lane + row * LANES < n_ref[0]).astype(F32)
        time = [(lax.rem(lane, TIMES) == t).astype(F32) for t in range(TIMES)]
        slot = lax.broadcasted_iota(jnp.int32, (slots, LANES), 0)
        hots, gains = [], []
        for end in range(2):
            hot = jnp.where(slot == slot_ref[row, end : end + 1], 1.0, 0.0).astype(BF16)
            hots.append(hot)
            g = jnp.dot(gain_ref[...], hot, preferred_element_type=F32)
            g = g[0:64] + g[64:128] + g[128:192]
            picked = sum(g[16 * t : 16 * t + 16] * time[t] for t in range(TIMES))
            gains.append([[picked[8 * part + 4 * pol : 8 * part + 4 * pol + 4] for pol in range(2)] for part in range(2)])
        sums = vis_ref[row]
        c = [sums[:, n] for n in range(4)]
        s = [sums[:, 4 + n] for n in range(4)]
        vis_r = [[c[0], c[1] + s[2]], [c[1] - s[2], c[3]]]
        vis_i = [[-s[0], c[2] - s[1]], [-c[2] - s[1], -s[3]]]
        (near_r, near_i), (far_r, far_i) = gains
        near = [[0.0, 0.0], [0.0, 0.0], [0.0, 0.0]]
        far = [[0.0, 0.0], [0.0, 0.0], [0.0, 0.0]]
        for a in range(2):
            for b in range(2):
                vr, vi = vis_r[a][b], vis_i[a][b]
                zr = far_r[b] * vr + far_i[b] * vi
                zi = far_r[b] * vi - far_i[b] * vr
                yr = near_r[a] * vr - near_i[a] * vi
                yi = near_r[a] * vi + near_i[a] * vr
                mr = near_r[a] * zr - near_i[a] * zi
                mi = near_r[a] * zi + near_i[a] * zr
                at = (a * 2 + b) * 4
                rr = weight * (obs_ref[row, at : at + 4] - mr)
                ri = weight * (obs_ref[row, 16 + at : 16 + at + 4] - mi)
                res_ref[row, at : at + 4] = rr
                res_ref[row, 16 + at : 16 + at + 4] = ri
                near[0][a] += weight * (zr * zr + zi * zi)
                near[1][a] += zr * rr + zi * ri
                near[2][a] += zr * ri - zi * rr
                far[0][b] += weight * (yr * yr + yi * yi)
                far[1][b] += yr * rr + yi * ri
                far[2][b] += yi * rr - yr * ri
        terms = []
        for end in (near, far):
            flat = jnp.concatenate([end[k][pol] for k in range(3) for pol in range(2)], axis=0)
            whole = jnp.concatenate([flat * time[t] for t in range(TIMES)], axis=0)
            hi = whole.astype(BF16)
            lo = (whole - hi.astype(F32)).astype(BF16)
            terms.append(jnp.concatenate([hi, lo], axis=0))
        both = lax.dot_general(
            jnp.concatenate(hots, axis=1),
            jnp.concatenate(terms, axis=1),
            (((1,), (1,)), ((), ())),
            preferred_element_type=F32,
        )
        norm_ref[...] += both
        return carry

    lax.fori_loop(0, (n_ref[0] + LANES - 1) // LANES, block, 0)


def calibrate(live, slots, vis, observed, gain):
    row_blocks = vis.shape[0]
    vmem = pl.BlockSpec(memory_space=pltpu.VMEM)
    res, norm = pl.pallas_call(
        calibrate_kernel,
        out_shape=(
            jax.ShapeDtypeStruct((row_blocks, 32, LANES), F32),
            jax.ShapeDtypeStruct((gain.shape[1], 192), F32),
        ),
        in_specs=[pl.BlockSpec(memory_space=pltpu.SMEM), vmem, vmem, vmem, vmem],
        out_specs=(vmem, vmem),
        compiler_params=pltpu.CompilerParams(vmem_limit_bytes=24 << 20),
        name="calibrate",
    )(live, slots, vis, observed, gain)
    return res, norm[:, :96] + norm[:, 96:]


def swap(value, axis, bits):
    count = lax.axis_size(axis)
    return lax.ppermute(value, axis, [(d, d ^ bits) for d in range(count)])


def pick(value, index):
    return lax.dynamic_index_in_dim(value, index, 0, keepdims=False)


def exchange(value):
    me = lax.axis_index("comp")
    got = [pick(value, me)] + [swap(pick(value, me ^ b), "comp", b) for b in range(1, GROUP)]
    got = jnp.stack(got)
    return jnp.stack([pick(got, me ^ j) for j in range(GROUP)])


def gathered(value):
    me = lax.axis_index("comp")
    got = jnp.stack([value] + [swap(value, "comp", b) for b in range(1, GROUP)])
    return jnp.stack([pick(got, me ^ j) for j in range(GROUP)])


def packed(blocks, starts):
    width = blocks.shape[-1]
    out = jnp.zeros(blocks.shape[1:-1] + (GROUP * width,), blocks.dtype)
    for j in range(GROUP):
        out = lax.dynamic_update_slice_in_dim(out, blocks[j], starts[j], axis=out.ndim - 1)
    return out


def owner_slots(antenna_owner, per_owner):
    index = jnp.arange(antenna_owner.shape[0], dtype=jnp.int32)
    same = (antenna_owner[None, :] == antenna_owner[:, None]) & (index[None, :] < index[:, None])
    return antenna_owner * per_owner + jnp.sum(same.astype(jnp.int32), axis=1)


def row_slots(antennas, slots):
    index = jnp.arange(slots.shape[0], dtype=jnp.int32)
    return jnp.sum(jnp.where(antennas[..., None] == index, slots, 0), axis=-1)


def local(baseline_uvw, antenna_pair, row_count, comp_position, comp_flux, gain, antenna_owner, observed):
    rows = baseline_uvw.shape[1]
    antennas = antenna_owner.shape[0]
    lines = lax.axis_size("bl")
    per_owner = antennas // (lines * GROUP)
    me_comp, me_line = lax.axis_index("comp"), lax.axis_index("bl")
    row_blocks = GROUP * rows // LANES

    head = jnp.concatenate(
        [baseline_uvw, antenna_pair.astype(F32), jnp.broadcast_to(row_count.astype(F32)[:, None], (1, rows))]
    )
    heads = gathered(head)
    counts = heads[:, 5, 0].astype(jnp.int32)
    ends = jnp.cumsum(counts)
    starts = ends - counts
    live = ends[-1:]
    rows_of = packed(heads[:, :5], starts)

    sums = predict(live, rows_of[:3], comp_position, comp_flux)

    obs = observed.reshape(rows, 8, GROUP, 4).transpose(2, 1, 3, 0).reshape(GROUP, 32 * rows)
    part = gain.reshape(per_owner, 16, GROUP, 4).transpose(2, 1, 3, 0).reshape(GROUP, 64 * per_owner)
    got = exchange(jnp.concatenate([obs, part], axis=1))
    obs = packed(got[:, : 32 * rows].reshape(GROUP, 32, rows), starts)
    obs = obs.reshape(32, row_blocks, LANES).transpose(1, 0, 2)
    table = got[:, 32 * rows :].reshape(1, GROUP, 64, per_owner)
    bit = 1
    while bit < lines:
        other = swap(table, "bl", bit)
        upper = (me_line & bit) != 0
        table = jnp.concatenate([jnp.where(upper, other, table), jnp.where(upper, table, other)], axis=0)
        bit *= 2
    table = table.transpose(2, 0, 1, 3).reshape(64, antennas)
    table = jnp.concatenate(pieces(table, 3), axis=0)
    slots = row_slots(rows_of[3:5].astype(jnp.int32), owner_slots(antenna_owner, per_owner))
    slots = slots.reshape(2, row_blocks, LANES).transpose(1, 0, 2)

    core, chip = me_comp & 1, me_comp >> 1
    sums = sums.reshape((2, 2) + sums.shape[1:])
    half = lax.dynamic_index_in_dim(sums, core, 1, keepdims=False)
    half = half + swap(lax.dynamic_index_in_dim(sums, 1 - core, 1, keepdims=False), "comp", 1)
    vis = pick(half, chip) + swap(pick(half, 1 - chip), "comp", 2)

    res, norm = calibrate(live, slots, vis, obs, table)

    norm = norm.reshape(lines, GROUP * per_owner, 96)
    bit = 1
    while bit < lines:
        side = (me_line & bit) // bit
        norm = norm.reshape((-1, 2) + norm.shape[1:])
        norm = lax.dynamic_index_in_dim(norm, side, 1, keepdims=False) + swap(
            lax.dynamic_index_in_dim(norm, 1 - side, 1, keepdims=False), "bl", bit
        )
        bit *= 2
    norm = exchange(norm.reshape(GROUP, per_owner, 24, 4))
    normal = norm.transpose(1, 2, 0, 3).reshape(per_owner, 24 * CHANNELS)

    res = res.transpose(1, 0, 2).reshape(32, GROUP * rows)
    res = exchange(
        jnp.stack([lax.dynamic_slice_in_dim(res, starts[j], rows, axis=1) for j in range(GROUP)])
    )
    residual = res.reshape(GROUP, 8, 4, rows).transpose(3, 1, 0, 2).reshape(rows, 8 * CHANNELS)
    alive = jnp.arange(rows, dtype=jnp.int32)[:, None] < row_count[0]
    return (jnp.where(alive, residual, 0.0), normal)


def solution(mesh):
    rows = P(("bl", "comp"))
    return jax.shard_map(
        local,
        mesh=mesh,
        in_specs=(
            P(None, ("bl", "comp")),
            P(None, ("bl", "comp")),
            rows,
            P(None, "comp"),
            P(None, None, "comp"),
            P(("bl", "comp"), None),
            P(),
            P(("bl", "comp"), None),
        ),
        out_specs=(P(("bl", "comp"), None), P(("bl", "comp"), None)),
        check_vma=False,
    )
```

```python
import jax
import jax.numpy as jnp
from jax import lax
from jax.experimental import pallas as pl
from jax.experimental.pallas import tpu as pltpu
from jax.sharding import PartitionSpec as P

CHANNELS = 16
TIMES = 4
GROUP = 4
LANES = 256
DEPTH = 256
STRIP = 16
F32 = jnp.float32
BF16 = jnp.bfloat16

SIN = [4 * v for v in (4.4428679030304945, -7.307443421264523, 3.5947880783696866, -0.7843740306721513)]
COS = [4 * v for v in (1.4142040804669556, -6.977642056688728, 5.71523839383031, -1.7283486597599615)]
CENTRES = (1 + 3.5 / 32, 1 + 11.5 / 32)
HALF_STEP = 1 / 64
TERMS = ((0, 0), (0, 1), (0, 2), (1, 0), (1, 1), (2, 0))


def pieces(x, count):
    out = []
    for _ in range(count):
        piece = lax.reduce_precision(x, 8, 7)
        out.append(piece.astype(BF16))
        x = x - piece
    return out


def turn(x):
    r = x - jnp.round(x)
    q = r * r
    s = (((SIN[3] * q + SIN[2]) * q + SIN[1]) * q + SIN[0]) * r
    c = ((COS[3] * q + COS[2]) * q + COS[1]) * q + COS[0]
    return 16.0 - s * s, s * c


def factors(t):
    out = []
    for centre in CENTRES:
        for v in turn(t * centre):
            hi = jnp.round(v)
            out += [hi.astype(BF16), (v - hi).astype(BF16)]
    c, s = turn(t * HALF_STEP)
    twice = (c * c) * (4.0 / 256.0) - 2.0
    cs, ss = [c, (twice - 1.0) * c], [s, (twice + 1.0) * s]
    for _ in range(2):
        cs.append(twice * cs[-1] - cs[-2])
        ss.append(twice * ss[-1] - ss[-2])
    for pair in zip(cs, ss):
        for v in pair:
            hi = jnp.round(v)
            out += [hi.astype(BF16), (v - hi).astype(BF16), v.astype(BF16)]
    return out


FACTORS = 32


def group_rows(info_ref):
    me = info_ref[GROUP]
    counts = [info_ref[b] for b in range(GROUP)]
    starts = [
        sum(jnp.where((me ^ c) < (me ^ b), counts[c], 0) for c in range(GROUP)) for b in range(GROUP)
    ]
    return starts, counts, sum(counts)


def place(ref, value, start, count):
    block, off = lax.div(start, LANES), lax.rem(start, LANES)
    lane = lax.broadcasted_iota(jnp.int32, value.shape, 1)
    turned = pltpu.roll(value, off, 1)
    ref[block] = jnp.where((lane >= off) & (lane < off + count), turned, ref[block])
    ref[block + 1] = jnp.where((lane < off) & (lane + LANES < off + count), turned, ref[block + 1])


def taken(ref, start, count):
    block, off = lax.div(start, LANES), lax.rem(start, LANES)
    back = lax.rem(LANES - off, LANES)
    first, second = pltpu.roll(ref[block], back, 1), pltpu.roll(ref[block + 1], back, 1)
    lane = lax.broadcasted_iota(jnp.int32, first.shape, 1)
    return jnp.where(lane < count, jnp.where(lane < LANES - off, first, second), 0.0)


def predict_kernel(blocks, info_ref, h0, h1, h2, h3, l_ref, tab_ref, o_ref, fa, fb, tt, ta, tb, acc, rows_ref, u_ref):
    starts, counts, live = group_rows(info_ref)
    total = lax.div(live + LANES - 1, LANES) * blocks
    rows_ref[...] = jnp.zeros_like(rows_ref)
    for b, head in enumerate((h0, h1, h2, h3)):
        place(rows_ref, head[0:8], starts[b], counts[b])
    for row in range(u_ref.shape[0]):
        parts, rest = [], rows_ref[row]
        for _ in range(3):
            part = rest.astype(BF16).astype(F32)
            parts.append(part)
            rest = rest - part
        u_ref[row] = jnp.concatenate([parts[i] for i, _ in TERMS], axis=0).astype(BF16)

    def begin(index, table):
        index = jnp.minimum(index, total - 1)
        row, block = lax.div(index, blocks), lax.rem(index, blocks)
        comps = pl.ds(pl.multiple_of(block * DEPTH, DEPTH), DEPTH)
        tt[...] = jnp.dot(l_ref[comps, :], u_ref[row], preferred_element_type=F32)
        table[...] = tab_ref[block]

    def strip(j, f):
        rows = slice(j * STRIP, (j + 1) * STRIP)
        for i, v in enumerate(factors(tt[rows])):
            f[i, rows] = v

    def product(d, f, table):
        pair, which = d // 4, d % 4
        a, k = pair // 4, pair % 4
        x = 4 * a + (2 if which in (1, 2) else 0)
        y = 8 + 6 * k + (3 if which in (1, 3) else 0)
        hi = f[x] * f[y]
        lo = f[x + 1] * f[y + 2] + f[x] * f[y + 1]
        t = table[pair]
        acc[pair, which] += jnp.dot(t, hi, preferred_element_type=F32) + jnp.dot(
            t, lo, preferred_element_type=F32
        )

    strips = DEPTH // STRIP

    def step(f, g, table):
        done = 0
        for d in range(32):
            product(d, f, table)
            while done < (d + 1) * strips // 32:
                strip(done, g)
                done += 1

    def flush(row):
        sign = jnp.where(lax.broadcasted_iota(jnp.int32, (8, LANES), 0) < 4, -1.0, 1.0)
        for pair in range(8):
            a, k = pair // 4, pair % 4
            p = [(acc[pair, w, 0:8] + acc[pair, w, 8:16]) * (1.0 / 256.0) for w in range(4)]
            c = p[0] + sign * p[1]
            s = p[2] - sign * p[3]
            plus, minus = (2 * a + 1) ^ info_ref[GROUP], (2 * a) ^ info_ref[GROUP]
            o_ref[plus & 1, plus >> 1, row, k] = jnp.concatenate([c[0:4], s[0:4]], axis=0)
            o_ref[minus & 1, minus >> 1, row, 3 - k] = jnp.concatenate([c[4:8], s[4:8]], axis=0)
        acc[...] = jnp.zeros_like(acc)

    o_ref[...] = jnp.zeros_like(o_ref)
    acc[...] = jnp.zeros_like(acc)
    begin(0, ta)
    for j in range(strips):
        strip(j, fa)

    def body(i, carry):
        begin(2 * i + 1, tb)
        step(fa, fb, ta)
        begin(2 * i + 2, ta)
        step(fb, fa, tb)

        @pl.when(lax.rem(2 * i + 2, blocks) == 0)
        def _():
            flush(lax.div(2 * i, blocks))

        return carry

    lax.fori_loop(0, total // 2, body, 0)


def predict(info, heads, position, flux):
    comps = position.shape[1]
    row_blocks, blocks = GROUP, comps // DEPTH
    l_coord, m_coord = position[0], position[1]
    n_minus = jnp.sqrt(1.0 - l_coord * l_coord - m_coord * m_coord) - 1.0
    lp = pieces(jnp.pad(jnp.stack([l_coord, m_coord, n_minus]), ((0, 5), (0, 0))), 3)
    l = jnp.concatenate([lp[j] for _, j in TERMS]).T
    i, q, v, w = flux
    bright = jnp.stack([i + q, v, w, i - q], 1).reshape(2, 8, 4, comps)
    plus, minus = bright[:, 4:].reshape(8, 4, comps), bright[:, 3::-1].reshape(8, 4, comps)
    hi, lo = pieces(jnp.concatenate([plus, minus], 1), 2)
    table = jnp.concatenate([hi, lo], 1).reshape(8, 16, blocks, DEPTH).transpose(2, 0, 1, 3)
    vmem = pl.BlockSpec(memory_space=pltpu.VMEM)
    return pl.pallas_call(
        lambda *refs: predict_kernel(blocks, *refs),
        out_shape=jax.ShapeDtypeStruct((2, 2, row_blocks, 4, 8, LANES), F32),
        in_specs=[pl.BlockSpec(memory_space=pltpu.SMEM)] + [vmem] * 6,
        out_specs=vmem,
        scratch_shapes=[
            pltpu.VMEM((FACTORS, DEPTH, LANES), BF16),
            pltpu.VMEM((FACTORS, DEPTH, LANES), BF16),
            pltpu.VMEM((DEPTH, LANES), F32),
            pltpu.VMEM((8, 16, DEPTH), BF16),
            pltpu.VMEM((8, 16, DEPTH), BF16),
            pltpu.VMEM((8, 4, 16, LANES), F32),
            pltpu.VMEM((row_blocks + 1, 8, LANES), F32),
            pltpu.VMEM((row_blocks, 48, LANES), BF16),
        ],
        compiler_params=pltpu.CompilerParams(vmem_limit_bytes=40 << 20),
        cost_estimate=pl.CostEstimate(
            flops=64 * 16 * GROUP * LANES * comps, bytes_accessed=4 << 20, transcendentals=0
        ),
        name="predict",
    )(info, *heads, l, table)


def calibrate_kernel(info_ref, h0, h1, h2, h3, x0, x1, x2, x3, own_ref, near_ref, far_ref, table_ref, out_ref, sum_ref, res_ref, norm_ref, obs_ref, slot_ref, gain_ref):
    slots = norm_ref.shape[0]
    flip = info_ref[GROUP + 1]
    starts, counts, live = group_rows(info_ref)
    norm_ref[...] = jnp.zeros_like(norm_ref)
    res_ref[...] = jnp.zeros_like(res_ref)
    obs_ref[...] = jnp.zeros_like(obs_ref)
    slot_ref[...] = jnp.zeros_like(slot_ref)
    for b, (head, obs) in enumerate(zip((h0, h1, h2, h3), (x0, x1, x2, x3))):
        place(slot_ref, head[0:8], starts[b], counts[b])
        place(obs_ref, obs[...], starts[b], counts[b])
    rest = table_ref[...]
    for p in range(3):
        part = rest.astype(BF16)
        gain_ref[64 * p : 64 * p + 64] = part
        rest = rest - part.astype(F32)

    def block(row, carry):
        lane = lax.broadcasted_iota(jnp.int32, (1, LANES), 1)
        weight = (lane + row * LANES < live).astype(F32)
        time = [(lax.rem(lane, TIMES) == t).astype(F32) for t in range(TIMES)]
        slot = lax.broadcasted_iota(jnp.int32, (slots, LANES), 0)
        hots, gains = [], []
        for end in range(2):
            at = slot_ref[row, 3 + end : 4 + end].astype(jnp.int32)
            hots.append(jnp.where(slot == at, 1.0, 0.0).astype(BF16))
            hot = jnp.where(slot == (at ^ flip), 1.0, 0.0).astype(BF16)
            g = jnp.dot(gain_ref[...], hot, preferred_element_type=F32)
            g = g[0:64] + g[64:128] + g[128:192]
            picked = sum(g[16 * t : 16 * t + 16] * time[t] for t in range(TIMES))
            gains.append([[picked[8 * part + 4 * pol : 8 * part + 4 * pol + 4] for pol in range(2)] for part in range(2)])
        sums = own_ref[row] + near_ref[row] + far_ref[row]
        c = [sums[:, n] for n in range(4)]
        s = [sums[:, 4 + n] for n in range(4)]
        vis_r = [[c[0], c[1] + s[2]], [c[1] - s[2], c[3]]]
        vis_i = [[-s[0], c[2] - s[1]], [-c[2] - s[1], -s[3]]]
        (near_r, near_i), (far_r, far_i) = gains
        near = [[0.0, 0.0], [0.0, 0.0], [0.0, 0.0]]
        far = [[0.0, 0.0], [0.0, 0.0], [0.0, 0.0]]
        for a in range(2):
            for b in range(2):
                vr, vi = vis_r[a][b], vis_i[a][b]
                zr = far_r[b] * vr + far_i[b] * vi
                zi = far_r[b] * vi - far_i[b] * vr
                yr = near_r[a] * vr - near_i[a] * vi
                yi = near_r[a] * vi + near_i[a] * vr
                mr = near_r[a] * zr - near_i[a] * zi
                mi = near_r[a] * zi + near_i[a] * zr
                at = (a * 2 + b) * 4
                rr = weight * (obs_ref[row, at : at + 4] - mr)
                ri = weight * (obs_ref[row, 16 + at : 16 + at + 4] - mi)
                res_ref[row, at : at + 4] = rr
                res_ref[row, 16 + at : 16 + at + 4] = ri
                near[0][a] += weight * (zr * zr + zi * zi)
                near[1][a] += zr * rr + zi * ri
                near[2][a] += zr * ri - zi * rr
                far[0][b] += weight * (yr * yr + yi * yi)
                far[1][b] += yr * rr + yi * ri
                far[2][b] += yi * rr - yr * ri
        terms = []
        for end in (near, far):
            flat = jnp.concatenate([end[k][pol] for k in range(3) for pol in range(2)], axis=0)
            whole = jnp.concatenate([flat * time[t] for t in range(TIMES)], axis=0)
            hi = whole.astype(BF16)
            lo = (whole - hi.astype(F32)).astype(BF16)
            terms.append(jnp.concatenate([hi, lo], axis=0))
        both = lax.dot_general(
            jnp.concatenate(hots, axis=1),
            jnp.concatenate(terms, axis=1),
            (((1,), (1,)), ((), ())),
            preferred_element_type=F32,
        )
        norm_ref[...] += both
        return carry

    lax.fori_loop(0, lax.div(live + LANES - 1, LANES), block, 0)
    sum_ref[...] = norm_ref[:, :96] + norm_ref[:, 96:]
    for b in range(GROUP):
        out_ref[b] = taken(res_ref, starts[b], counts[b])


def calibrate(info, heads, obs, parts, table):
    antennas = table.shape[1]
    vmem = pl.BlockSpec(memory_space=pltpu.VMEM)
    return pl.pallas_call(
        calibrate_kernel,
        out_shape=(
            jax.ShapeDtypeStruct((GROUP, 32, LANES), F32),
            jax.ShapeDtypeStruct((antennas, 96), F32),
        ),
        in_specs=[pl.BlockSpec(memory_space=pltpu.SMEM)] + [vmem] * 12,
        out_specs=(vmem, vmem),
        scratch_shapes=[
            pltpu.VMEM((GROUP + 1, 32, LANES), F32),
            pltpu.VMEM((antennas, 192), F32),
            pltpu.VMEM((GROUP + 1, 32, LANES), F32),
            pltpu.VMEM((GROUP + 1, 8, LANES), F32),
            pltpu.VMEM((192, antennas), BF16),
        ],
        compiler_params=pltpu.CompilerParams(vmem_limit_bytes=24 << 20),
        name="calibrate",
    )(info, *heads, *obs, *parts, table)


def swap(value, axis, bits):
    count = lax.axis_size(axis)
    return lax.ppermute(value, axis, [(d, d ^ bits) for d in range(count)])


def relative(values, core, chip):
    values = [jnp.where(core, values[j ^ 1], values[j]) for j in range(GROUP)]
    return [jnp.where(chip, values[j ^ 2], values[j]) for j in range(GROUP)]


def exchange(values):
    return [values[0]] + [swap(values[b], "comp", b) for b in range(1, GROUP)]


def owner_slots(antenna_owner, per_owner):
    index = jnp.arange(antenna_owner.shape[0], dtype=jnp.int32)
    same = (antenna_owner[None, :] == antenna_owner[:, None]) & (index[None, :] < index[:, None])
    return antenna_owner * per_owner + jnp.sum(same.astype(jnp.int32), axis=1)


def row_slots(antennas, slots):
    index = jnp.arange(slots.shape[0], dtype=jnp.int32)
    return jnp.sum(jnp.where(antennas[..., None] == index, slots, 0), axis=-1)


def local(baseline_uvw, antenna_pair, row_count, comp_position, comp_flux, gain, antenna_owner, observed):
    rows = baseline_uvw.shape[1]
    antennas = antenna_owner.shape[0]
    lines = lax.axis_size("bl")
    per_owner = antennas // (lines * GROUP)
    me_comp, me_line = lax.axis_index("comp"), lax.axis_index("bl")
    core, chip = (me_comp & 1) != 0, me_comp >= 2

    slots = row_slots(antenna_pair, owner_slots(antenna_owner, per_owner))
    count = jnp.broadcast_to(row_count[:, None], (3, rows))
    head = jnp.concatenate([baseline_uvw, slots.astype(F32), count.astype(F32)])
    part = gain.reshape(per_owner, 16, GROUP, 4).transpose(2, 1, 3, 0).reshape(GROUP, -1, rows)
    part = relative(list(part), core, chip)
    heads = exchange([jnp.concatenate([head, p]) for p in part])
    counts = [h[5:6, 0].astype(jnp.int32) for h in heads]
    flip = (me_line * GROUP + me_comp) * per_owner
    info = jnp.concatenate(counts + [jnp.stack([me_comp, flip]).astype(jnp.int32)])

    obs = observed.reshape(rows, 8, GROUP, 4).transpose(2, 1, 3, 0).reshape(GROUP, 32, rows)
    obs = exchange(relative(list(obs), core, chip))

    mine = jnp.concatenate([h[8:] for h in heads])
    even = jnp.stack([mine] + [swap(mine, "bl", b) for b in range(2, lines, 2)])

    sums = predict(info, heads, comp_position, comp_flux)

    first = swap(sums[1], "comp", 1)
    odd = swap(even, "bl", 1)
    second = swap(sums[0, 1] + first[1], "comp", 2)
    table = jnp.stack([even, odd], 1).reshape(lines, GROUP, 64, per_owner)
    table = table.transpose(2, 0, 1, 3).reshape(64, antennas)

    res, norm = calibrate(info, heads, obs, (sums[0, 0], first[0], second), table)

    res = exchange(list(res))
    norm = lax.all_to_all(norm.reshape(lines * GROUP, per_owner, 96), ("bl", "comp"), 0, 0)
    norm = jnp.sum(norm.reshape(lines, GROUP, per_owner, 24, 4), axis=0)
    normal = norm.transpose(1, 2, 0, 3).reshape(per_owner, 24 * CHANNELS)
    res = jnp.stack(relative(res, core, chip))
    residual = res.reshape(GROUP, 8, 4, rows).transpose(3, 1, 0, 2).reshape(rows, 8 * CHANNELS)
    return (residual, normal)


def solution(mesh):
    rows = P(("bl", "comp"))
    return jax.shard_map(
        local,
        mesh=mesh,
        in_specs=(
            P(None, ("bl", "comp")),
            P(None, ("bl", "comp")),
            rows,
            P(None, "comp"),
            P(None, None, "comp"),
            P(("bl", "comp"), None),
            P(),
            P(("bl", "comp"), None),
        ),
        out_specs=(P(("bl", "comp"), None), P(("bl", "comp"), None)),
        check_vma=False,
    )
```

```python
import jax
import jax.numpy as jnp
from jax import lax
from jax.experimental import pallas as pl
from jax.experimental.pallas import tpu as pltpu
from jax.sharding import PartitionSpec as P

CHANNELS = 16
TIMES = 4
GROUP = 4
LANES = 256
DEPTH = 256
STRIP = 16
F32 = jnp.float32
BF16 = jnp.bfloat16

SIN = [4 * v for v in (4.4428679030304945, -7.307443421264523, 3.5947880783696866, -0.7843740306721513)]
COS = [4 * v for v in (1.4142040804669556, -6.977642056688728, 5.71523839383031, -1.7283486597599615)]
CENTRES = (1 + 3.5 / 32, 1 + 11.5 / 32)
HALF_STEP = 1 / 64
TERMS = ((0, 0), (0, 1), (0, 2), (1, 0), (1, 1), (2, 0))


def pieces(x, count):
    out = []
    for _ in range(count):
        piece = lax.reduce_precision(x, 8, 7)
        out.append(piece.astype(BF16))
        x = x - piece
    return out


def turn(x):
    r = x - jnp.round(x)
    q = r * r
    s = (((SIN[3] * q + SIN[2]) * q + SIN[1]) * q + SIN[0]) * r
    c = ((COS[3] * q + COS[2]) * q + COS[1]) * q + COS[0]
    return 16.0 - s * s, s * c


def factors(t, put):
    for a, centre in enumerate(CENTRES):
        pair = turn(t * centre)
        yield
        for m, v in enumerate(pair):
            hi = jnp.round(v)
            for n, part in enumerate((hi, v - hi, v)):
                put(6 * a + 3 * m + n, part.astype(BF16))
        yield
    c, s = turn(t * HALF_STEP)
    yield
    twice = (c * c) * (4.0 / 256.0) - 2.0
    cs, ss = [c, (twice - 1.0) * c], [s, (twice + 1.0) * s]
    for k in range(4):
        if k > 1:
            cs.append(twice * cs[-1] - cs[-2])
            ss.append(twice * ss[-1] - ss[-2])
        for m, v in enumerate((cs[k], ss[k])):
            hi = jnp.round(v)
            put(12 + 4 * k + 2 * m, hi.astype(BF16))
            put(13 + 4 * k + 2 * m, (v - hi).astype(BF16))
        yield


FACTORS = 28
PIECES = 9


def group_rows(info_ref, heads):
    me = info_ref[0]
    counts = [jnp.max(head[5:6, 0:128]).astype(jnp.int32) for head in heads]
    starts = [
        sum(jnp.where((me ^ c) < (me ^ b), counts[c], 0) for c in range(GROUP)) for b in range(GROUP)
    ]
    return starts, counts, sum(counts)


def place(ref, value, start, count):
    block, off = lax.div(start, LANES), lax.rem(start, LANES)
    lane = lax.broadcasted_iota(jnp.int32, value.shape, 1)
    turned = pltpu.roll(value, off, 1)
    ref[block] = jnp.where((lane >= off) & (lane < off + count), turned, ref[block])
    ref[block + 1] = jnp.where((lane < off) & (lane + LANES < off + count), turned, ref[block + 1])


def taken(ref, start, count):
    block, off = lax.div(start, LANES), lax.rem(start, LANES)
    back = lax.rem(LANES - off, LANES)
    first, second = pltpu.roll(ref[block], back, 1), pltpu.roll(ref[block + 1], back, 1)
    lane = lax.broadcasted_iota(jnp.int32, first.shape, 1)
    return jnp.where(lane < count, jnp.where(lane < LANES - off, first, second), 0.0)


def predict_kernel(blocks, info_ref, h0, h1, h2, h3, l_ref, tab_ref, o_ref, fa, fb, tt, ta, tb, acc, rows_ref, u_ref):
    starts, counts, live = group_rows(info_ref, (h0, h1, h2, h3))
    total = lax.div(live + LANES - 1, LANES) * blocks
    rows_ref[...] = jnp.zeros_like(rows_ref)
    for b, head in enumerate((h0, h1, h2, h3)):
        place(rows_ref, head[0:8], starts[b], counts[b])
    for row in range(u_ref.shape[0]):
        parts, rest = [], rows_ref[row]
        for _ in range(3):
            part = rest.astype(BF16).astype(F32)
            parts.append(part)
            rest = rest - part
        u_ref[row] = jnp.concatenate([parts[i] for i, _ in TERMS], axis=0).astype(BF16)

    def begin(index, table):
        index = jnp.minimum(index, total - 1)
        row, block = lax.div(index, blocks), lax.rem(index, blocks)
        comps = pl.ds(pl.multiple_of(block * DEPTH, DEPTH), DEPTH)
        tt[...] = jnp.dot(l_ref[comps, :], u_ref[row], preferred_element_type=F32)
        table[...] = tab_ref[block]

    def strips(f):
        for j in range(DEPTH // STRIP):
            rows = slice(j * STRIP, (j + 1) * STRIP)

            def put(i, v, rows=rows):
                f[i, rows] = v

            yield from factors(tt[rows], put)

    def product(d, f, table):
        pair, which = d // 4, d % 4
        a, k = pair // 4, pair % 4
        x = 6 * a + (3 if which in (1, 2) else 0)
        y = 12 + 4 * k + (2 if which in (1, 3) else 0)
        t = table[pair]
        hi = f[x] * f[y]
        both = jnp.dot(t, hi, preferred_element_type=F32)
        yield
        lo = f[x + 1] * f[y] + f[x + 2] * f[y + 1]
        both += jnp.dot(t, lo, preferred_element_type=F32)
        yield
        acc[pair, which] += both

    def step(f, g, table):
        ahead, done, count = strips(g), 0, 0
        for d in range(32):
            for _ in product(d, f, table):
                count += 1
                while done < count * PIECES * (DEPTH // STRIP) // 64:
                    next(ahead, None)
                    done += 1
        for _ in ahead:
            pass

    def flush(row):
        sign = jnp.where(lax.broadcasted_iota(jnp.int32, (8, LANES), 0) < 4, -1.0, 1.0)
        for pair in range(8):
            a, k = pair // 4, pair % 4
            p = [(acc[pair, w, 0:8] + acc[pair, w, 8:16]) * (1.0 / 256.0) for w in range(4)]
            c = p[0] + sign * p[1]
            s = p[2] - sign * p[3]
            plus, minus = (2 * a + 1) ^ info_ref[0], (2 * a) ^ info_ref[0]
            o_ref[plus & 1, plus >> 1, row, k] = jnp.concatenate([c[0:4], s[0:4]], axis=0)
            o_ref[minus & 1, minus >> 1, row, 3 - k] = jnp.concatenate([c[4:8], s[4:8]], axis=0)
        acc[...] = jnp.zeros_like(acc)

    o_ref[...] = jnp.zeros_like(o_ref)
    acc[...] = jnp.zeros_like(acc)
    begin(0, ta)
    for _ in strips(fa):
        pass

    def body(i, carry):
        begin(2 * i + 1, tb)
        step(fa, fb, ta)
        begin(2 * i + 2, ta)
        step(fb, fa, tb)

        @pl.when(lax.rem(2 * i + 2, blocks) == 0)
        def _():
            flush(lax.div(2 * i, blocks))

        return carry

    lax.fori_loop(0, total // 2, body, 0)


def predict(info, heads, position, flux):
    comps = position.shape[1]
    row_blocks, blocks = GROUP, comps // DEPTH
    l_coord, m_coord = position[0], position[1]
    n_minus = jnp.sqrt(1.0 - l_coord * l_coord - m_coord * m_coord) - 1.0
    lp = pieces(jnp.pad(jnp.stack([l_coord, m_coord, n_minus]), ((0, 5), (0, 0))), 3)
    l = jnp.concatenate([lp[j] for _, j in TERMS]).T
    i, q, v, w = flux
    bright = jnp.stack([i + q, v, w, i - q], 1).reshape(2, 8, 4, comps)
    plus, minus = bright[:, 4:].reshape(8, 4, comps), bright[:, 3::-1].reshape(8, 4, comps)
    hi, lo = pieces(jnp.concatenate([plus, minus], 1), 2)
    table = jnp.concatenate([hi, lo], 1).reshape(8, 16, blocks, DEPTH).transpose(2, 0, 1, 3)
    vmem = pl.BlockSpec(memory_space=pltpu.VMEM)
    return pl.pallas_call(
        lambda *refs: predict_kernel(blocks, *refs),
        out_shape=jax.ShapeDtypeStruct((2, 2, row_blocks, 4, 8, LANES), F32),
        in_specs=[pl.BlockSpec(memory_space=pltpu.SMEM)] + [vmem] * 6,
        out_specs=vmem,
        scratch_shapes=[
            pltpu.VMEM((FACTORS, DEPTH, LANES), BF16),
            pltpu.VMEM((FACTORS, DEPTH, LANES), BF16),
            pltpu.VMEM((DEPTH, LANES), F32),
            pltpu.VMEM((8, 16, DEPTH), BF16),
            pltpu.VMEM((8, 16, DEPTH), BF16),
            pltpu.VMEM((8, 4, 16, LANES), F32),
            pltpu.VMEM((row_blocks + 1, 8, LANES), F32),
            pltpu.VMEM((row_blocks, 48, LANES), BF16),
        ],
        compiler_params=pltpu.CompilerParams(vmem_limit_bytes=40 << 20),
        cost_estimate=pl.CostEstimate(
            flops=64 * 16 * GROUP * LANES * comps, bytes_accessed=4 << 20, transcendentals=0
        ),
        name="predict",
    )(info, *heads, l, table)


def prepare_kernel(info_ref, h0, h1, h2, h3, table_ref, obs_ref, slot_ref, picked_ref, gain_ref):
    slots = table_ref.shape[1]
    flip = info_ref[1]
    starts, counts, live = group_rows(info_ref, (h0, h1, h2, h3))
    obs_ref[...] = jnp.zeros_like(obs_ref)
    slot_ref[...] = jnp.zeros_like(slot_ref)
    for b, head in enumerate((h0, h1, h2, h3)):
        place(slot_ref, head[0:8], starts[b], counts[b])
        place(obs_ref, head[8:40], starts[b], counts[b])
    rest = table_ref[...]
    for p in range(3):
        part = rest.astype(BF16)
        gain_ref[64 * p : 64 * p + 64] = part
        rest = rest - part.astype(F32)

    def block(row, carry):
        lane = lax.broadcasted_iota(jnp.int32, (1, LANES), 1)
        time = [(lax.rem(lane, TIMES) == t).astype(F32) for t in range(TIMES)]
        slot = lax.broadcasted_iota(jnp.int32, (slots, LANES), 0)
        for end in range(2):
            at = slot_ref[row, 3 + end : 4 + end].astype(jnp.int32)
            hot = jnp.where(slot == (at ^ flip), 1.0, 0.0).astype(BF16)
            g = jnp.dot(gain_ref[...], hot, preferred_element_type=F32)
            g = g[0:64] + g[64:128] + g[128:192]
            picked_ref[row, end] = sum(g[16 * t : 16 * t + 16] * time[t] for t in range(TIMES))
        return carry

    lax.fori_loop(0, lax.div(live + LANES - 1, LANES), block, 0)


def calibrate_kernel(info_ref, h0, h1, h2, h3, obs_ref, slot_ref, picked_ref, own_ref, near_ref, far_ref, out_ref, sum_ref, res_ref, norm_ref):
    slots = norm_ref.shape[0]
    starts, counts, live = group_rows(info_ref, (h0, h1, h2, h3))
    norm_ref[...] = jnp.zeros_like(norm_ref)
    res_ref[...] = jnp.zeros_like(res_ref)

    def block(row, carry):
        lane = lax.broadcasted_iota(jnp.int32, (1, LANES), 1)
        weight = (lane + row * LANES < live).astype(F32)
        time = [(lax.rem(lane, TIMES) == t).astype(F32) for t in range(TIMES)]
        slot = lax.broadcasted_iota(jnp.int32, (slots, LANES), 0)
        hots, gains = [], []
        for end in range(2):
            at = slot_ref[row, 3 + end : 4 + end].astype(jnp.int32)
            hots.append(jnp.where(slot == at, 1.0, 0.0).astype(BF16))
            picked = picked_ref[row, end]
            gains.append([[picked[8 * part + 4 * pol : 8 * part + 4 * pol + 4] for pol in range(2)] for part in range(2)])
        sums = own_ref[row] + near_ref[row] + far_ref[row]
        c = [sums[:, n] for n in range(4)]
        s = [sums[:, 4 + n] for n in range(4)]
        vis_r = [[c[0], c[1] + s[2]], [c[1] - s[2], c[3]]]
        vis_i = [[-s[0], c[2] - s[1]], [-c[2] - s[1], -s[3]]]
        (near_r, near_i), (far_r, far_i) = gains
        near = [[0.0, 0.0], [0.0, 0.0], [0.0, 0.0]]
        far = [[0.0, 0.0], [0.0, 0.0], [0.0, 0.0]]
        for a in range(2):
            for b in range(2):
                vr, vi = vis_r[a][b], vis_i[a][b]
                zr = far_r[b] * vr + far_i[b] * vi
                zi = far_r[b] * vi - far_i[b] * vr
                yr = near_r[a] * vr - near_i[a] * vi
                yi = near_r[a] * vi + near_i[a] * vr
                mr = near_r[a] * zr - near_i[a] * zi
                mi = near_r[a] * zi + near_i[a] * zr
                at = (a * 2 + b) * 4
                rr = weight * (obs_ref[row, at : at + 4] - mr)
                ri = weight * (obs_ref[row, 16 + at : 16 + at + 4] - mi)
                res_ref[row, at : at + 4] = rr
                res_ref[row, 16 + at : 16 + at + 4] = ri
                near[0][a] += weight * (zr * zr + zi * zi)
                near[1][a] += zr * rr + zi * ri
                near[2][a] += zr * ri - zi * rr
                far[0][b] += weight * (yr * yr + yi * yi)
                far[1][b] += yr * rr + yi * ri
                far[2][b] += yi * rr - yr * ri
        terms = []
        for end in (near, far):
            flat = jnp.concatenate([end[k][pol] for k in range(3) for pol in range(2)], axis=0)
            whole = jnp.concatenate([flat * time[t] for t in range(TIMES)], axis=0)
            hi = whole.astype(BF16)
            lo = (whole - hi.astype(F32)).astype(BF16)
            terms.append(jnp.concatenate([hi, lo], axis=0))
        both = lax.dot_general(
            jnp.concatenate(hots, axis=1),
            jnp.concatenate(terms, axis=1),
            (((1,), (1,)), ((), ())),
            preferred_element_type=F32,
        )
        norm_ref[...] += both
        return carry

    lax.fori_loop(0, lax.div(live + LANES - 1, LANES), block, 0)
    sum_ref[...] = norm_ref[:, :96] + norm_ref[:, 96:]
    for b in range(GROUP):
        out_ref[b] = taken(res_ref, starts[b], counts[b])


VMEM = pl.BlockSpec(memory_space=pltpu.VMEM)
SMEM = pl.BlockSpec(memory_space=pltpu.SMEM)


def prepare(info, heads, table):
    return pl.pallas_call(
        prepare_kernel,
        out_shape=(
            jax.ShapeDtypeStruct((GROUP + 1, 32, LANES), F32),
            jax.ShapeDtypeStruct((GROUP + 1, 8, LANES), F32),
            jax.ShapeDtypeStruct((GROUP, 2, 16, LANES), F32),
        ),
        in_specs=[SMEM] + [VMEM] * 5,
        out_specs=(VMEM, VMEM, VMEM),
        scratch_shapes=[pltpu.VMEM((192, table.shape[1]), BF16)],
        compiler_params=pltpu.CompilerParams(vmem_limit_bytes=16 << 20),
        cost_estimate=pl.CostEstimate(flops=1 << 30, bytes_accessed=1 << 20, transcendentals=0),
        name="prepare",
    )(info, *heads, table)


def calibrate(info, heads, ready, parts, antennas):
    return pl.pallas_call(
        calibrate_kernel,
        out_shape=(
            jax.ShapeDtypeStruct((GROUP, 32, LANES), F32),
            jax.ShapeDtypeStruct((antennas, 96), F32),
        ),
        in_specs=[SMEM] + [VMEM] * 10,
        out_specs=(VMEM, VMEM),
        scratch_shapes=[
            pltpu.VMEM((GROUP + 1, 32, LANES), F32),
            pltpu.VMEM((antennas, 192), F32),
        ],
        compiler_params=pltpu.CompilerParams(vmem_limit_bytes=24 << 20),
        name="calibrate",
    )(info, *heads, *ready, *parts)


def swap(value, axis, bits):
    count = lax.axis_size(axis)
    return lax.ppermute(value, axis, [(d, d ^ bits) for d in range(count)])


def relative(values, core, chip):
    values = [jnp.where(core, values[j ^ 1], values[j]) for j in range(GROUP)]
    return [jnp.where(chip, values[j ^ 2], values[j]) for j in range(GROUP)]


def exchange(values):
    return [values[0]] + [swap(values[b], "comp", b) for b in range(1, GROUP)]


def owner_slots(antenna_owner, per_owner):
    index = jnp.arange(antenna_owner.shape[0], dtype=jnp.int32)
    same = (antenna_owner[None, :] == antenna_owner[:, None]) & (index[None, :] < index[:, None])
    return antenna_owner * per_owner + jnp.sum(same.astype(jnp.int32), axis=1)


def row_slots(antennas, slots):
    index = jnp.arange(slots.shape[0], dtype=jnp.int32)
    return jnp.sum(jnp.where(antennas[..., None] == index, slots, 0), axis=-1)


def local(baseline_uvw, antenna_pair, row_count, comp_position, comp_flux, gain, antenna_owner, observed):
    rows = baseline_uvw.shape[1]
    antennas = antenna_owner.shape[0]
    lines = lax.axis_size("bl")
    per_owner = antennas // (lines * GROUP)
    me_comp, me_line = lax.axis_index("comp"), lax.axis_index("bl")
    core, chip = (me_comp & 1) != 0, me_comp >= 2

    slots = row_slots(antenna_pair, owner_slots(antenna_owner, per_owner))
    count = jnp.broadcast_to(row_count[:, None], (3, rows))
    head = jnp.concatenate([baseline_uvw, slots.astype(F32), count.astype(F32)])
    part = gain.reshape(per_owner, 16, GROUP, 4).transpose(2, 1, 3, 0).reshape(GROUP, -1, rows)
    part = relative(list(part), core, chip)
    obs = observed.reshape(rows, 8, GROUP, 4).transpose(2, 1, 3, 0).reshape(GROUP, 32, rows)
    obs = relative(list(obs), core, chip)
    heads = exchange([jnp.concatenate([head, o, p]) for o, p in zip(obs, part)])
    info = jnp.stack([me_comp, (me_line * GROUP + me_comp) * per_owner]).astype(jnp.int32)

    mine = jnp.concatenate([h[40:] for h in heads])
    even = jnp.stack([mine] + [swap(mine, "bl", b) for b in range(2, lines, 2)])

    sums = predict(info, heads, comp_position, comp_flux)

    first = swap(sums[1], "comp", 1)
    odd = swap(even, "bl", 1)
    half = sums[0, 1] + first[1]
    second = swap(half, "comp", 2)
    odd, _ = lax.optimization_barrier((odd, half))
    table = jnp.stack([even, odd], 1).reshape(lines, GROUP, 64, per_owner)
    table = table.transpose(2, 0, 1, 3).reshape(64, antennas)

    ready = prepare(info, heads, table)
    res, norm = calibrate(info, heads, ready, (sums[0, 0], first[0], second), antennas)

    res = exchange(list(res))
    norm = lax.all_to_all(norm.reshape(lines * GROUP, per_owner, 96), ("bl", "comp"), 0, 0)
    norm = jnp.sum(norm.reshape(lines, GROUP, per_owner, 24, 4), axis=0)
    normal = norm.transpose(1, 2, 0, 3).reshape(per_owner, 24 * CHANNELS)
    res = jnp.stack(relative(res, core, chip))
    residual = res.reshape(GROUP, 8, 4, rows).transpose(3, 1, 0, 2).reshape(rows, 8 * CHANNELS)
    return (residual, normal)


def solution(mesh):
    rows = P(("bl", "comp"))
    return jax.shard_map(
        local,
        mesh=mesh,
        in_specs=(
            P(None, ("bl", "comp")),
            P(None, ("bl", "comp")),
            rows,
            P(None, "comp"),
            P(None, None, "comp"),
            P(("bl", "comp"), None),
            P(),
            P(("bl", "comp"), None),
        ),
        out_specs=(P(("bl", "comp"), None), P(("bl", "comp"), None)),
        check_vma=False,
    )
```

```python
import jax
import jax.numpy as jnp
from jax import lax
from jax.experimental import pallas as pl
from jax.experimental.pallas import tpu as pltpu
from jax.sharding import PartitionSpec as P

CHANNELS = 16
TIMES = 4
GROUP = 4
LANES = 256
DEPTH = 256
STRIP = 16
F32 = jnp.float32
BF16 = jnp.bfloat16

SIN = [4 * v for v in (4.4428679030304945, -7.307443421264523, 3.5947880783696866, -0.7843740306721513)]
COS = [4 * v for v in (1.4142040804669556, -6.977642056688728, 5.71523839383031, -1.7283486597599615)]
CENTRES = (1 + 3.5 / 32, 1 + 11.5 / 32)
HALF_STEP = 1 / 64
TERMS = ((0, 0), (0, 1), (0, 2), (1, 0), (1, 1), (2, 0))


def pieces(x, count):
    out = []
    for _ in range(count):
        piece = lax.reduce_precision(x, 8, 7)
        out.append(piece.astype(BF16))
        x = x - piece
    return out


def turn(x):
    r = x - jnp.round(x)
    q = r * r
    s = (((SIN[3] * q + SIN[2]) * q + SIN[1]) * q + SIN[0]) * r
    c = ((COS[3] * q + COS[2]) * q + COS[1]) * q + COS[0]
    return 16.0 - s * s, s * c


def factors(t, put):
    for a, centre in enumerate(CENTRES):
        pair = turn(t * centre)
        yield
        for m, v in enumerate(pair):
            hi = jnp.round(v)
            for n, part in enumerate((hi, v - hi, v)):
                put(6 * a + 3 * m + n, part.astype(BF16))
        yield
    c, s = turn(t * HALF_STEP)
    yield
    twice = (c * c) * (4.0 / 256.0) - 2.0
    cs, ss = [c, (twice - 1.0) * c], [s, (twice + 1.0) * s]
    for k in range(4):
        if k > 1:
            cs.append(twice * cs[-1] - cs[-2])
            ss.append(twice * ss[-1] - ss[-2])
        for m, v in enumerate((cs[k], ss[k])):
            hi = jnp.round(v)
            put(12 + 4 * k + 2 * m, hi.astype(BF16))
            put(13 + 4 * k + 2 * m, (v - hi).astype(BF16))
        yield


FACTORS = 28
PIECES = 9


def group_rows(info_ref, heads):
    me = info_ref[0]
    counts = [jnp.max(head[5:6, 0:128]).astype(jnp.int32) for head in heads]
    starts = [
        sum(jnp.where((me ^ c) < (me ^ b), counts[c], 0) for c in range(GROUP)) for b in range(GROUP)
    ]
    return starts, counts, sum(counts)


def place(ref, value, start, count):
    block, off = lax.div(start, LANES), lax.rem(start, LANES)
    lane = lax.broadcasted_iota(jnp.int32, value.shape, 1)
    turned = pltpu.roll(value, off, 1)
    ref[block] = jnp.where((lane >= off) & (lane < off + count), turned, ref[block])
    ref[block + 1] = jnp.where((lane < off) & (lane + LANES < off + count), turned, ref[block + 1])


def taken(ref, start, count):
    block, off = lax.div(start, LANES), lax.rem(start, LANES)
    back = lax.rem(LANES - off, LANES)
    first, second = pltpu.roll(ref[block], back, 1), pltpu.roll(ref[block + 1], back, 1)
    lane = lax.broadcasted_iota(jnp.int32, first.shape, 1)
    return jnp.where(lane < count, jnp.where(lane < LANES - off, first, second), 0.0)


def predict_kernel(blocks, info_ref, h0, h1, h2, h3, l_ref, tab_ref, o_ref, fa, fb, tt, ta, tb, acc, acc2, rows_ref, u_ref):
    starts, counts, live = group_rows(info_ref, (h0, h1, h2, h3))
    half = LANES // 2
    rest_rows = lax.rem(live, LANES)
    halved = (rest_rows > 0) & (rest_rows <= half)
    full = lax.div(live + half - 1, LANES)
    total = full * blocks
    last = total + jnp.where(halved, blocks // 2, 0) - 1
    rows_ref[...] = jnp.zeros_like(rows_ref)
    for b, head in enumerate((h0, h1, h2, h3)):
        place(rows_ref, head[0:8], starts[b], counts[b])
    for row in range(u_ref.shape[0]):
        parts, rest = [], rows_ref[row]
        for _ in range(3):
            part = rest.astype(BF16).astype(F32)
            parts.append(part)
            rest = rest - part
        u = jnp.concatenate([parts[i] for i, _ in TERMS], axis=0).astype(BF16)
        u_ref[row, 0] = u[:, :half]
        u_ref[row, 1] = u[:, half:]

    def begin(index, table):
        index = jnp.minimum(index, last)
        extra = index - total
        pair = extra >= 0
        row = jnp.where(pair, full, lax.div(index, blocks))
        left = jnp.where(pair, 2 * extra, lax.rem(index, blocks))
        right = jnp.where(pair, left + 1, left)
        for side, block in enumerate((left, right)):
            comps = pl.ds(pl.multiple_of(block * DEPTH, DEPTH), DEPTH)
            u = u_ref[row, jnp.where(pair, 0, side)]
            tt[:, side * half : side * half + half] = jnp.dot(l_ref[comps, :], u, preferred_element_type=F32)
            table[:, 16 * side : 16 * side + 16] = tab_ref[block]

    def strips(f):
        for j in range(DEPTH // STRIP):
            rows = slice(j * STRIP, (j + 1) * STRIP)

            def put(i, v, rows=rows):
                f[i, rows] = v

            yield from factors(tt[rows], put)

    def product(d, f, table, into):
        pair, which = d // 4, d % 4
        a, k = pair // 4, pair % 4
        x = 6 * a + (3 if which in (1, 2) else 0)
        y = 12 + 4 * k + (2 if which in (1, 3) else 0)
        t = table[pair, 0 : into.shape[2]]
        hi = f[x] * f[y]
        both = jnp.dot(t, hi, preferred_element_type=F32)
        yield
        lo = f[x + 1] * f[y] + f[x + 2] * f[y + 1]
        both += jnp.dot(t, lo, preferred_element_type=F32)
        yield
        into[pair, which] += both

    def step(f, g, table, into):
        ahead, done, count = strips(g), 0, 0
        for d in range(32):
            for _ in product(d, f, table, into):
                count += 1
                while done < count * PIECES * (DEPTH // STRIP) // 64:
                    next(ahead, None)
                    done += 1
        for _ in ahead:
            pass

    def flush(row):
        sign = jnp.where(lax.broadcasted_iota(jnp.int32, (8, LANES), 0) < 4, -1.0, 1.0)
        for pair in range(8):
            a, k = pair // 4, pair % 4
            p = [(acc[pair, w, 0:8] + acc[pair, w, 8:16]) * (1.0 / 256.0) for w in range(4)]
            c = p[0] + sign * p[1]
            s = p[2] - sign * p[3]
            plus, minus = (2 * a + 1) ^ info_ref[0], (2 * a) ^ info_ref[0]
            o_ref[plus & 1, plus >> 1, row, k] = jnp.concatenate([c[0:4], s[0:4]], axis=0)
            o_ref[minus & 1, minus >> 1, row, 3 - k] = jnp.concatenate([c[4:8], s[4:8]], axis=0)
        acc[...] = jnp.zeros_like(acc)

    o_ref[...] = jnp.zeros_like(o_ref)
    acc[...] = jnp.zeros_like(acc)
    begin(0, ta)
    for _ in strips(fa):
        pass

    def twice(first, into):
        begin(first + 1, tb)
        step(fa, fb, ta, into)
        begin(first + 2, ta)
        step(fb, fa, tb, into)

    def body(i, carry):
        twice(2 * i, acc)

        @pl.when(lax.rem(2 * i + 2, blocks) == 0)
        def _():
            flush(lax.div(2 * i, blocks))

        return carry

    lax.fori_loop(0, total // 2, body, 0)

    @pl.when(halved)
    def _():
        acc2[...] = jnp.zeros_like(acc2)

        def body2(i, carry):
            twice(total + 2 * i, acc2)
            return carry

        lax.fori_loop(0, blocks // 4, body2, 0)
        for pair in range(8):
            for w in range(4):
                z = acc2[pair, w, 0:16, :half] + acc2[pair, w, 16:32, half:]
                acc[pair, w] = jnp.concatenate([z, jnp.zeros_like(z)], axis=1)
        flush(full)


def predict(info, heads, position, flux):
    comps = position.shape[1]
    row_blocks, blocks = GROUP, comps // DEPTH
    l_coord, m_coord = position[0], position[1]
    n_minus = jnp.sqrt(1.0 - l_coord * l_coord - m_coord * m_coord) - 1.0
    lp = pieces(jnp.pad(jnp.stack([l_coord, m_coord, n_minus]), ((0, 5), (0, 0))), 3)
    l = jnp.concatenate([lp[j] for _, j in TERMS]).T
    i, q, v, w = flux
    bright = jnp.stack([i + q, v, w, i - q], 1).reshape(2, 8, 4, comps)
    plus, minus = bright[:, 4:].reshape(8, 4, comps), bright[:, 3::-1].reshape(8, 4, comps)
    hi, lo = pieces(jnp.concatenate([plus, minus], 1), 2)
    table = jnp.concatenate([hi, lo], 1).reshape(8, 16, blocks, DEPTH).transpose(2, 0, 1, 3)
    vmem = pl.BlockSpec(memory_space=pltpu.VMEM)
    return pl.pallas_call(
        lambda *refs: predict_kernel(blocks, *refs),
        out_shape=jax.ShapeDtypeStruct((2, 2, row_blocks, 4, 8, LANES), F32),
        in_specs=[pl.BlockSpec(memory_space=pltpu.SMEM)] + [vmem] * 6,
        out_specs=vmem,
        scratch_shapes=[
            pltpu.VMEM((FACTORS, DEPTH, LANES), BF16),
            pltpu.VMEM((FACTORS, DEPTH, LANES), BF16),
            pltpu.VMEM((DEPTH, LANES), F32),
            pltpu.VMEM((8, 32, DEPTH), BF16),
            pltpu.VMEM((8, 32, DEPTH), BF16),
            pltpu.VMEM((8, 4, 16, LANES), F32),
            pltpu.VMEM((8, 4, 32, LANES), F32),
            pltpu.VMEM((row_blocks + 1, 8, LANES), F32),
            pltpu.VMEM((row_blocks, 2, 48, LANES // 2), BF16),
        ],
        compiler_params=pltpu.CompilerParams(vmem_limit_bytes=40 << 20),
        cost_estimate=pl.CostEstimate(
            flops=64 * 16 * GROUP * LANES * comps, bytes_accessed=4 << 20, transcendentals=0
        ),
        name="predict",
    )(info, *heads, l, table)


def prepare_kernel(info_ref, h0, h1, h2, h3, table_ref, obs_ref, slot_ref, picked_ref, gain_ref):
    slots = table_ref.shape[1]
    flip = info_ref[1]
    starts, counts, live = group_rows(info_ref, (h0, h1, h2, h3))
    obs_ref[...] = jnp.zeros_like(obs_ref)
    slot_ref[...] = jnp.zeros_like(slot_ref)
    for b, head in enumerate((h0, h1, h2, h3)):
        place(slot_ref, head[0:8], starts[b], counts[b])
        place(obs_ref, head[8:40], starts[b], counts[b])
    rest = table_ref[...]
    for p in range(3):
        part = rest.astype(BF16)
        gain_ref[64 * p : 64 * p + 64] = part
        rest = rest - part.astype(F32)

    def block(row, carry):
        lane = lax.broadcasted_iota(jnp.int32, (1, LANES), 1)
        time = [(lax.rem(lane, TIMES) == t).astype(F32) for t in range(TIMES)]
        slot = lax.broadcasted_iota(jnp.int32, (slots, LANES), 0)
        for end in range(2):
            at = slot_ref[row, 3 + end : 4 + end].astype(jnp.int32)
            hot = jnp.where(slot == (at ^ flip), 1.0, 0.0).astype(BF16)
            g = jnp.dot(gain_ref[...], hot, preferred_element_type=F32)
            g = g[0:64] + g[64:128] + g[128:192]
            picked_ref[row, end] = sum(g[16 * t : 16 * t + 16] * time[t] for t in range(TIMES))
        return carry

    lax.fori_loop(0, lax.div(live + LANES - 1, LANES), block, 0)


def calibrate_kernel(info_ref, h0, h1, h2, h3, obs_ref, slot_ref, picked_ref, own_ref, near_ref, far_ref, out_ref, sum_ref, res_ref, norm_ref):
    slots = norm_ref.shape[0]
    starts, counts, live = group_rows(info_ref, (h0, h1, h2, h3))
    norm_ref[...] = jnp.zeros_like(norm_ref)
    res_ref[...] = jnp.zeros_like(res_ref)

    def block(row, carry):
        lane = lax.broadcasted_iota(jnp.int32, (1, LANES), 1)
        weight = (lane + row * LANES < live).astype(F32)
        time = [(lax.rem(lane, TIMES) == t).astype(F32) for t in range(TIMES)]
        slot = lax.broadcasted_iota(jnp.int32, (slots, LANES), 0)
        hots, gains = [], []
        for end in range(2):
            at = slot_ref[row, 3 + end : 4 + end].astype(jnp.int32)
            hots.append(jnp.where(slot == at, 1.0, 0.0).astype(BF16))
            picked = picked_ref[row, end]
            gains.append([[picked[8 * part + 4 * pol : 8 * part + 4 * pol + 4] for pol in range(2)] for part in range(2)])
        sums = own_ref[row] + near_ref[row] + far_ref[row]
        c = [sums[:, n] for n in range(4)]
        s = [sums[:, 4 + n] for n in range(4)]
        vis_r = [[c[0], c[1] + s[2]], [c[1] - s[2], c[3]]]
        vis_i = [[-s[0], c[2] - s[1]], [-c[2] - s[1], -s[3]]]
        (near_r, near_i), (far_r, far_i) = gains
        near = [[0.0, 0.0], [0.0, 0.0], [0.0, 0.0]]
        far = [[0.0, 0.0], [0.0, 0.0], [0.0, 0.0]]
        for a in range(2):
            for b in range(2):
                vr, vi = vis_r[a][b], vis_i[a][b]
                zr = far_r[b] * vr + far_i[b] * vi
                zi = far_r[b] * vi - far_i[b] * vr
                yr = near_r[a] * vr - near_i[a] * vi
                yi = near_r[a] * vi + near_i[a] * vr
                mr = near_r[a] * zr - near_i[a] * zi
                mi = near_r[a] * zi + near_i[a] * zr
                at = (a * 2 + b) * 4
                rr = weight * (obs_ref[row, at : at + 4] - mr)
                ri = weight * (obs_ref[row, 16 + at : 16 + at + 4] - mi)
                res_ref[row, at : at + 4] = rr
                res_ref[row, 16 + at : 16 + at + 4] = ri
                near[0][a] += weight * (zr * zr + zi * zi)
                near[1][a] += zr * rr + zi * ri
                near[2][a] += zr * ri - zi * rr
                far[0][b] += weight * (yr * yr + yi * yi)
                far[1][b] += yr * rr + yi * ri
                far[2][b] += yi * rr - yr * ri
        terms = []
        for end in (near, far):
            flat = jnp.concatenate([end[k][pol] for k in range(3) for pol in range(2)], axis=0)
            whole = jnp.concatenate([flat * time[t] for t in range(TIMES)], axis=0)
            hi = whole.astype(BF16)
            lo = (whole - hi.astype(F32)).astype(BF16)
            terms.append(jnp.concatenate([hi, lo], axis=0))
        both = lax.dot_general(
            jnp.concatenate(hots, axis=1),
            jnp.concatenate(terms, axis=1),
            (((1,), (1,)), ((), ())),
            preferred_element_type=F32,
        )
        norm_ref[...] += both
        return carry

    lax.fori_loop(0, lax.div(live + LANES - 1, LANES), block, 0)
    sum_ref[...] = norm_ref[:, :96] + norm_ref[:, 96:]
    for b in range(GROUP):
        out_ref[b] = taken(res_ref, starts[b], counts[b])


VMEM = pl.BlockSpec(memory_space=pltpu.VMEM)
SMEM = pl.BlockSpec(memory_space=pltpu.SMEM)


def prepare(info, heads, table):
    return pl.pallas_call(
        prepare_kernel,
        out_shape=(
            jax.ShapeDtypeStruct((GROUP + 1, 32, LANES), F32),
            jax.ShapeDtypeStruct((GROUP + 1, 8, LANES), F32),
            jax.ShapeDtypeStruct((GROUP, 2, 16, LANES), F32),
        ),
        in_specs=[SMEM] + [VMEM] * 5,
        out_specs=(VMEM, VMEM, VMEM),
        scratch_shapes=[pltpu.VMEM((192, table.shape[1]), BF16)],
        compiler_params=pltpu.CompilerParams(vmem_limit_bytes=16 << 20),
        cost_estimate=pl.CostEstimate(flops=1 << 30, bytes_accessed=1 << 20, transcendentals=0),
        name="prepare",
    )(info, *heads, table)


def calibrate(info, heads, ready, parts, antennas):
    return pl.pallas_call(
        calibrate_kernel,
        out_shape=(
            jax.ShapeDtypeStruct((GROUP, 32, LANES), F32),
            jax.ShapeDtypeStruct((antennas, 96), F32),
        ),
        in_specs=[SMEM] + [VMEM] * 10,
        out_specs=(VMEM, VMEM),
        scratch_shapes=[
            pltpu.VMEM((GROUP + 1, 32, LANES), F32),
            pltpu.VMEM((antennas, 192), F32),
        ],
        compiler_params=pltpu.CompilerParams(vmem_limit_bytes=24 << 20),
        name="calibrate",
    )(info, *heads, *ready, *parts)


def swap(value, axis, bits):
    count = lax.axis_size(axis)
    return lax.ppermute(value, axis, [(d, d ^ bits) for d in range(count)])


def relative(values, core, chip):
    values = [jnp.where(core, values[j ^ 1], values[j]) for j in range(GROUP)]
    return [jnp.where(chip, values[j ^ 2], values[j]) for j in range(GROUP)]


def exchange(values):
    return [values[0]] + [swap(values[b], "comp", b) for b in range(1, GROUP)]


def owner_slots(antenna_owner, per_owner):
    index = jnp.arange(antenna_owner.shape[0], dtype=jnp.int32)
    same = (antenna_owner[None, :] == antenna_owner[:, None]) & (index[None, :] < index[:, None])
    return antenna_owner * per_owner + jnp.sum(same.astype(jnp.int32), axis=1)


def row_slots(antennas, slots):
    index = jnp.arange(slots.shape[0], dtype=jnp.int32)
    return jnp.sum(jnp.where(antennas[..., None] == index, slots, 0), axis=-1)


def local(baseline_uvw, antenna_pair, row_count, comp_position, comp_flux, gain, antenna_owner, observed):
    rows = baseline_uvw.shape[1]
    antennas = antenna_owner.shape[0]
    lines = lax.axis_size("bl")
    per_owner = antennas // (lines * GROUP)
    me_comp, me_line = lax.axis_index("comp"), lax.axis_index("bl")
    core, chip = (me_comp & 1) != 0, me_comp >= 2

    slots = row_slots(antenna_pair, owner_slots(antenna_owner, per_owner))
    count = jnp.broadcast_to(row_count[:, None], (3, rows))
    head = jnp.concatenate([baseline_uvw, slots.astype(F32), count.astype(F32)])
    part = gain.reshape(per_owner, 16, GROUP, 4).transpose(2, 1, 3, 0).reshape(GROUP, -1, rows)
    part = relative(list(part), core, chip)
    obs = observed.reshape(rows, 8, GROUP, 4).transpose(2, 1, 3, 0).reshape(GROUP, 32, rows)
    obs = relative(list(obs), core, chip)
    heads = exchange([jnp.concatenate([head, o, p]) for o, p in zip(obs, part)])
    info = jnp.stack([me_comp, (me_line * GROUP + me_comp) * per_owner]).astype(jnp.int32)

    mine = jnp.concatenate([h[40:] for h in heads])
    even = jnp.stack([mine] + [swap(mine, "bl", b) for b in range(2, lines, 2)])

    sums = predict(info, heads, comp_position, comp_flux)

    first = swap(sums[1], "comp", 1)
    odd = swap(even, "bl", 1)
    half = sums[0, 1] + first[1]
    second = swap(half, "comp", 2)
    odd, _ = lax.optimization_barrier((odd, half))
    table = jnp.stack([even, odd], 1).reshape(lines, GROUP, 64, per_owner)
    table = table.transpose(2, 0, 1, 3).reshape(64, antennas)

    ready = prepare(info, heads, table)
    res, norm = calibrate(info, heads, ready, (sums[0, 0], first[0], second), antennas)

    res = exchange(list(res))
    norm = lax.all_to_all(norm.reshape(lines * GROUP, per_owner, 96), ("bl", "comp"), 0, 0)
    norm = jnp.sum(norm.reshape(lines, GROUP, per_owner, 24, 4), axis=0)
    normal = norm.transpose(1, 2, 0, 3).reshape(per_owner, 24 * CHANNELS)
    res = jnp.stack(relative(res, core, chip))
    residual = res.reshape(GROUP, 8, 4, rows).transpose(3, 1, 0, 2).reshape(rows, 8 * CHANNELS)
    return (residual, normal)


def solution(mesh):
    rows = P(("bl", "comp"))
    return jax.shard_map(
        local,
        mesh=mesh,
        in_specs=(
            P(None, ("bl", "comp")),
            P(None, ("bl", "comp")),
            rows,
            P(None, "comp"),
            P(None, None, "comp"),
            P(("bl", "comp"), None),
            P(),
            P(("bl", "comp"), None),
        ),
        out_specs=(P(("bl", "comp"), None), P(("bl", "comp"), None)),
        check_vma=False,
    )
```

```python
import jax
import jax.numpy as jnp
from jax import lax
from jax.experimental import pallas as pl
from jax.experimental.pallas import tpu as pltpu
from jax.sharding import PartitionSpec as P

CHANNELS = 16
TIMES = 4
GROUP = 4
LANES = 256
DEPTH = 256
STRIP = 16
F32 = jnp.float32
BF16 = jnp.bfloat16

SIN = [4 * v for v in (4.4428679030304945, -7.307443421264523, 3.5947880783696866, -0.7843740306721513)]
COS = [4 * v for v in (1.4142040804669556, -6.977642056688728, 5.71523839383031, -1.7283486597599615)]
CENTRES = (1 + 3.5 / 32, 1 + 11.5 / 32)
HALF_STEP = 1 / 64
TERMS = ((0, 0), (0, 1), (0, 2), (1, 0), (1, 1), (2, 0))


def pieces(x, count):
    out = []
    for _ in range(count):
        piece = lax.reduce_precision(x, 8, 7)
        out.append(piece.astype(BF16))
        x = x - piece
    return out


def turn(x):
    r = x - jnp.round(x)
    q = r * r
    s = (((SIN[3] * q + SIN[2]) * q + SIN[1]) * q + SIN[0]) * r
    c = ((COS[3] * q + COS[2]) * q + COS[1]) * q + COS[0]
    return 16.0 - s * s, s * c


def factors(t, put):
    for a, centre in enumerate(CENTRES):
        pair = turn(t * centre)
        yield
        for m, v in enumerate(pair):
            hi = jnp.round(v)
            for n, part in enumerate((hi, v - hi, v)):
                put(6 * a + 3 * m + n, part.astype(BF16))
        yield
    c, s = turn(t * HALF_STEP)
    yield
    twice = (c * c) * (4.0 / 256.0) - 2.0
    cs, ss = [c, (twice - 1.0) * c], [s, (twice + 1.0) * s]
    for k in range(4):
        if k > 1:
            cs.append(twice * cs[-1] - cs[-2])
            ss.append(twice * ss[-1] - ss[-2])
        for m, v in enumerate((cs[k], ss[k])):
            hi = jnp.round(v)
            put(12 + 4 * k + 2 * m, hi.astype(BF16))
            put(13 + 4 * k + 2 * m, (v - hi).astype(BF16))
        yield


FACTORS = 28
PIECES = 9


def group_rows(info_ref, heads):
    me = info_ref[0]
    counts = [jnp.max(head[5:6, 0:128]).astype(jnp.int32) for head in heads]
    starts = [
        sum(jnp.where((me ^ c) < (me ^ b), counts[c], 0) for c in range(GROUP)) for b in range(GROUP)
    ]
    return starts, counts, sum(counts)


def place(ref, value, start, count):
    block, off = lax.div(start, LANES), lax.rem(start, LANES)
    lane = lax.broadcasted_iota(jnp.int32, value.shape, 1)
    turned = pltpu.roll(value, off, 1)
    ref[block] = jnp.where((lane >= off) & (lane < off + count), turned, ref[block])
    ref[block + 1] = jnp.where((lane < off) & (lane + LANES < off + count), turned, ref[block + 1])


def taken(ref, start, count):
    block, off = lax.div(start, LANES), lax.rem(start, LANES)
    back = lax.rem(LANES - off, LANES)
    first, second = pltpu.roll(ref[block], back, 1), pltpu.roll(ref[block + 1], back, 1)
    lane = lax.broadcasted_iota(jnp.int32, first.shape, 1)
    return jnp.where(lane < count, jnp.where(lane < LANES - off, first, second), 0.0)


def predict_kernel(blocks, info_ref, h0, h1, h2, h3, l_ref, tab_ref, o_ref, fa, fb, tt, ta, tb, acc, acc2, rows_ref, u_ref):
    starts, counts, live = group_rows(info_ref, (h0, h1, h2, h3))
    half = LANES // 2
    rest_rows = lax.rem(live, LANES)
    halved = (rest_rows > 0) & (rest_rows <= half)
    full = lax.div(live + half - 1, LANES)
    total = full * blocks
    rows_ref[...] = jnp.zeros_like(rows_ref)
    for b, head in enumerate((h0, h1, h2, h3)):
        place(rows_ref, head[0:8], starts[b], counts[b])
    for row in range(u_ref.shape[0]):
        parts, rest = [], rows_ref[row]
        for _ in range(3):
            part = rest.astype(BF16).astype(F32)
            parts.append(part)
            rest = rest - part
        u_ref[row] = jnp.concatenate([parts[i] for i, _ in TERMS], axis=0).astype(BF16)

    def depth(block):
        return pl.ds(pl.multiple_of(block * DEPTH, DEPTH), DEPTH)

    def begin(index, table):
        index = jnp.clip(index, 0, jnp.maximum(total - 1, 0))
        row, block = lax.div(index, blocks), lax.rem(index, blocks)
        tt[...] = jnp.dot(l_ref[depth(block), :], u_ref[row], preferred_element_type=F32)
        table[:, 0:16] = tab_ref[block]

    def begin_halved(index, table):
        index = jnp.minimum(index, blocks // 2 - 1)
        for side in range(2):
            block = 2 * index + side
            tt[:, side * half : side * half + half] = jnp.dot(
                l_ref[depth(block), :], u_ref[full, :, :half], preferred_element_type=F32
            )
            table[:, 16 * side : 16 * side + 16] = tab_ref[block]

    def strips(f):
        for j in range(DEPTH // STRIP):
            rows = slice(j * STRIP, (j + 1) * STRIP)

            def put(i, v, rows=rows):
                f[i, rows] = v

            yield from factors(tt[rows], put)

    def product(d, f, table, into):
        pair, which = d // 4, d % 4
        a, k = pair // 4, pair % 4
        x = 6 * a + (3 if which in (1, 2) else 0)
        y = 12 + 4 * k + (2 if which in (1, 3) else 0)
        t = table[pair, 0 : into.shape[2]]
        hi = f[x] * f[y]
        both = jnp.dot(t, hi, preferred_element_type=F32)
        yield
        lo = f[x + 1] * f[y] + f[x + 2] * f[y + 1]
        both += jnp.dot(t, lo, preferred_element_type=F32)
        yield
        into[pair, which] += both

    def step(f, g, table, into):
        ahead, done, count = strips(g), 0, 0
        for d in range(32):
            for _ in product(d, f, table, into):
                count += 1
                while done < count * PIECES * (DEPTH // STRIP) // 64:
                    next(ahead, None)
                    done += 1
        for _ in ahead:
            pass

    def flush(row):
        sign = jnp.where(lax.broadcasted_iota(jnp.int32, (8, LANES), 0) < 4, -1.0, 1.0)
        for pair in range(8):
            a, k = pair // 4, pair % 4
            p = [(acc[pair, w, 0:8] + acc[pair, w, 8:16]) * (1.0 / 256.0) for w in range(4)]
            c = p[0] + sign * p[1]
            s = p[2] - sign * p[3]
            plus, minus = (2 * a + 1) ^ info_ref[0], (2 * a) ^ info_ref[0]
            o_ref[plus & 1, plus >> 1, row, k] = jnp.concatenate([c[0:4], s[0:4]], axis=0)
            o_ref[minus & 1, minus >> 1, row, 3 - k] = jnp.concatenate([c[4:8], s[4:8]], axis=0)
        acc[...] = jnp.zeros_like(acc)

    o_ref[...] = jnp.zeros_like(o_ref)
    acc[...] = jnp.zeros_like(acc)

    def first(start):
        start(0, ta)
        for _ in strips(fa):
            pass

    def twice(start, index, into):
        start(index + 1, tb)
        step(fa, fb, ta, into)
        start(index + 2, ta)
        step(fb, fa, tb, into)

    first(begin)

    def body(i, carry):
        twice(begin, 2 * i, acc)

        @pl.when(lax.rem(2 * i + 2, blocks) == 0)
        def _():
            flush(lax.div(2 * i, blocks))

        return carry

    lax.fori_loop(0, total // 2, body, 0)

    @pl.when(halved)
    def _():
        acc2[...] = jnp.zeros_like(acc2)
        first(begin_halved)

        def body2(i, carry):
            twice(begin_halved, 2 * i, acc2)
            return carry

        lax.fori_loop(0, blocks // 4, body2, 0)
        for pair in range(8):
            for w in range(4):
                z = acc2[pair, w, 0:16, :half] + acc2[pair, w, 16:32, half:]
                acc[pair, w] = jnp.concatenate([z, jnp.zeros_like(z)], axis=1)
        flush(full)


def predict(info, heads, position, flux):
    comps = position.shape[1]
    row_blocks, blocks = GROUP, comps // DEPTH
    l_coord, m_coord = position[0], position[1]
    n_minus = jnp.sqrt(1.0 - l_coord * l_coord - m_coord * m_coord) - 1.0
    lp = pieces(jnp.pad(jnp.stack([l_coord, m_coord, n_minus]), ((0, 5), (0, 0))), 3)
    l = jnp.concatenate([lp[j] for _, j in TERMS]).T
    i, q, v, w = flux
    bright = jnp.stack([i + q, v, w, i - q], 1).reshape(2, 8, 4, comps)
    plus, minus = bright[:, 4:].reshape(8, 4, comps), bright[:, 3::-1].reshape(8, 4, comps)
    hi, lo = pieces(jnp.concatenate([plus, minus], 1), 2)
    table = jnp.concatenate([hi, lo], 1).reshape(8, 16, blocks, DEPTH).transpose(2, 0, 1, 3)
    vmem = pl.BlockSpec(memory_space=pltpu.VMEM)
    return pl.pallas_call(
        lambda *refs: predict_kernel(blocks, *refs),
        out_shape=jax.ShapeDtypeStruct((2, 2, row_blocks, 4, 8, LANES), F32),
        in_specs=[pl.BlockSpec(memory_space=pltpu.SMEM)] + [vmem] * 6,
        out_specs=vmem,
        scratch_shapes=[
            pltpu.VMEM((FACTORS, DEPTH, LANES), BF16),
            pltpu.VMEM((FACTORS, DEPTH, LANES), BF16),
            pltpu.VMEM((DEPTH, LANES), F32),
            pltpu.VMEM((8, 32, DEPTH), BF16),
            pltpu.VMEM((8, 32, DEPTH), BF16),
            pltpu.VMEM((8, 4, 16, LANES), F32),
            pltpu.VMEM((8, 4, 32, LANES), F32),
            pltpu.VMEM((row_blocks + 1, 8, LANES), F32),
            pltpu.VMEM((row_blocks, 48, LANES), BF16),
        ],
        compiler_params=pltpu.CompilerParams(vmem_limit_bytes=40 << 20),
        cost_estimate=pl.CostEstimate(
            flops=64 * 16 * GROUP * LANES * comps, bytes_accessed=4 << 20, transcendentals=0
        ),
        name="predict",
    )(info, *heads, l, table)


def prepare_kernel(info_ref, h0, h1, h2, h3, table_ref, obs_ref, slot_ref, picked_ref, gain_ref):
    slots = table_ref.shape[1]
    flip = info_ref[1]
    starts, counts, live = group_rows(info_ref, (h0, h1, h2, h3))
    obs_ref[...] = jnp.zeros_like(obs_ref)
    slot_ref[...] = jnp.zeros_like(slot_ref)
    for b, head in enumerate((h0, h1, h2, h3)):
        place(slot_ref, head[0:8], starts[b], counts[b])
        place(obs_ref, head[8:40], starts[b], counts[b])
    rest = table_ref[...]
    for p in range(3):
        part = rest.astype(BF16)
        gain_ref[64 * p : 64 * p + 64] = part
        rest = rest - part.astype(F32)

    def block(row, carry):
        lane = lax.broadcasted_iota(jnp.int32, (1, LANES), 1)
        time = [(lax.rem(lane, TIMES) == t).astype(F32) for t in range(TIMES)]
        slot = lax.broadcasted_iota(jnp.int32, (slots, LANES), 0)
        for end in range(2):
            at = slot_ref[row, 3 + end : 4 + end].astype(jnp.int32)
            hot = jnp.where(slot == (at ^ flip), 1.0, 0.0).astype(BF16)
            g = jnp.dot(gain_ref[...], hot, preferred_element_type=F32)
            g = g[0:64] + g[64:128] + g[128:192]
            picked_ref[row, end] = sum(g[16 * t : 16 * t + 16] * time[t] for t in range(TIMES))
        return carry

    lax.fori_loop(0, lax.div(live + LANES - 1, LANES), block, 0)


def calibrate_kernel(info_ref, h0, h1, h2, h3, obs_ref, slot_ref, picked_ref, own_ref, near_ref, far_ref, out_ref, sum_ref, res_ref, norm_ref):
    slots = norm_ref.shape[0]
    starts, counts, live = group_rows(info_ref, (h0, h1, h2, h3))
    norm_ref[...] = jnp.zeros_like(norm_ref)
    res_ref[...] = jnp.zeros_like(res_ref)

    def block(row, carry):
        lane = lax.broadcasted_iota(jnp.int32, (1, LANES), 1)
        weight = (lane + row * LANES < live).astype(F32)
        time = [(lax.rem(lane, TIMES) == t).astype(F32) for t in range(TIMES)]
        slot = lax.broadcasted_iota(jnp.int32, (slots, LANES), 0)
        hots, gains = [], []
        for end in range(2):
            at = slot_ref[row, 3 + end : 4 + end].astype(jnp.int32)
            hots.append(jnp.where(slot == at, 1.0, 0.0).astype(BF16))
            picked = picked_ref[row, end]
            gains.append([[picked[8 * part + 4 * pol : 8 * part + 4 * pol + 4] for pol in range(2)] for part in range(2)])
        sums = own_ref[row] + near_ref[row] + far_ref[row]
        c = [sums[:, n] for n in range(4)]
        s = [sums[:, 4 + n] for n in range(4)]
        vis_r = [[c[0], c[1] + s[2]], [c[1] - s[2], c[3]]]
        vis_i = [[-s[0], c[2] - s[1]], [-c[2] - s[1], -s[3]]]
        (near_r, near_i), (far_r, far_i) = gains
        near = [[0.0, 0.0], [0.0, 0.0], [0.0, 0.0]]
        far = [[0.0, 0.0], [0.0, 0.0], [0.0, 0.0]]
        for a in range(2):
            for b in range(2):
                vr, vi = vis_r[a][b], vis_i[a][b]
                zr = far_r[b] * vr + far_i[b] * vi
                zi = far_r[b] * vi - far_i[b] * vr
                yr = near_r[a] * vr - near_i[a] * vi
                yi = near_r[a] * vi + near_i[a] * vr
                mr = near_r[a] * zr - near_i[a] * zi
                mi = near_r[a] * zi + near_i[a] * zr
                at = (a * 2 + b) * 4
                rr = weight * (obs_ref[row, at : at + 4] - mr)
                ri = weight * (obs_ref[row, 16 + at : 16 + at + 4] - mi)
                res_ref[row, at : at + 4] = rr
                res_ref[row, 16 + at : 16 + at + 4] = ri
                near[0][a] += weight * (zr * zr + zi * zi)
                near[1][a] += zr * rr + zi * ri
                near[2][a] += zr * ri - zi * rr
                far[0][b] += weight * (yr * yr + yi * yi)
                far[1][b] += yr * rr + yi * ri
                far[2][b] += yi * rr - yr * ri
        terms = []
        for end in (near, far):
            flat = jnp.concatenate([end[k][pol] for k in range(3) for pol in range(2)], axis=0)
            whole = jnp.concatenate([flat * time[t] for t in range(TIMES)], axis=0)
            hi = whole.astype(BF16)
            lo = (whole - hi.astype(F32)).astype(BF16)
            terms.append(jnp.concatenate([hi, lo], axis=0))
        both = lax.dot_general(
            jnp.concatenate(hots, axis=1),
            jnp.concatenate(terms, axis=1),
            (((1,), (1,)), ((), ())),
            preferred_element_type=F32,
        )
        norm_ref[...] += both
        return carry

    lax.fori_loop(0, lax.div(live + LANES - 1, LANES), block, 0)
    sum_ref[...] = norm_ref[:, :96] + norm_ref[:, 96:]
    for b in range(GROUP):
        out_ref[b] = taken(res_ref, starts[b], counts[b])


VMEM = pl.BlockSpec(memory_space=pltpu.VMEM)
SMEM = pl.BlockSpec(memory_space=pltpu.SMEM)


def prepare(info, heads, table):
    return pl.pallas_call(
        prepare_kernel,
        out_shape=(
            jax.ShapeDtypeStruct((GROUP + 1, 32, LANES), F32),
            jax.ShapeDtypeStruct((GROUP + 1, 8, LANES), F32),
            jax.ShapeDtypeStruct((GROUP, 2, 16, LANES), F32),
        ),
        in_specs=[SMEM] + [VMEM] * 5,
        out_specs=(VMEM, VMEM, VMEM),
        scratch_shapes=[pltpu.VMEM((192, table.shape[1]), BF16)],
        compiler_params=pltpu.CompilerParams(vmem_limit_bytes=16 << 20),
        cost_estimate=pl.CostEstimate(flops=1 << 30, bytes_accessed=1 << 20, transcendentals=0),
        name="prepare",
    )(info, *heads, table)


def calibrate(info, heads, ready, parts, antennas):
    return pl.pallas_call(
        calibrate_kernel,
        out_shape=(
            jax.ShapeDtypeStruct((GROUP, 32, LANES), F32),
            jax.ShapeDtypeStruct((antennas, 96), F32),
        ),
        in_specs=[SMEM] + [VMEM] * 10,
        out_specs=(VMEM, VMEM),
        scratch_shapes=[
            pltpu.VMEM((GROUP + 1, 32, LANES), F32),
            pltpu.VMEM((antennas, 192), F32),
        ],
        compiler_params=pltpu.CompilerParams(vmem_limit_bytes=24 << 20),
        name="calibrate",
    )(info, *heads, *ready, *parts)


def swap(value, axis, bits):
    count = lax.axis_size(axis)
    return lax.ppermute(value, axis, [(d, d ^ bits) for d in range(count)])


def relative(values, core, chip):
    values = [jnp.where(core, values[j ^ 1], values[j]) for j in range(GROUP)]
    return [jnp.where(chip, values[j ^ 2], values[j]) for j in range(GROUP)]


def exchange(values):
    return [values[0]] + [swap(values[b], "comp", b) for b in range(1, GROUP)]


def owner_slots(antenna_owner, per_owner):
    index = jnp.arange(antenna_owner.shape[0], dtype=jnp.int32)
    same = (antenna_owner[None, :] == antenna_owner[:, None]) & (index[None, :] < index[:, None])
    return antenna_owner * per_owner + jnp.sum(same.astype(jnp.int32), axis=1)


def row_slots(antennas, slots):
    index = jnp.arange(slots.shape[0], dtype=jnp.int32)
    return jnp.sum(jnp.where(antennas[..., None] == index, slots, 0), axis=-1)


def local(baseline_uvw, antenna_pair, row_count, comp_position, comp_flux, gain, antenna_owner, observed):
    rows = baseline_uvw.shape[1]
    antennas = antenna_owner.shape[0]
    lines = lax.axis_size("bl")
    per_owner = antennas // (lines * GROUP)
    me_comp, me_line = lax.axis_index("comp"), lax.axis_index("bl")
    core, chip = (me_comp & 1) != 0, me_comp >= 2

    slots = row_slots(antenna_pair, owner_slots(antenna_owner, per_owner))
    count = jnp.broadcast_to(row_count[:, None], (3, rows))
    head = jnp.concatenate([baseline_uvw, slots.astype(F32), count.astype(F32)])
    part = gain.reshape(per_owner, 16, GROUP, 4).transpose(2, 1, 3, 0).reshape(GROUP, -1, rows)
    part = relative(list(part), core, chip)
    obs = observed.reshape(rows, 8, GROUP, 4).transpose(2, 1, 3, 0).reshape(GROUP, 32, rows)
    obs = relative(list(obs), core, chip)
    heads = exchange([jnp.concatenate([head, o, p]) for o, p in zip(obs, part)])
    info = jnp.stack([me_comp, (me_line * GROUP + me_comp) * per_owner]).astype(jnp.int32)

    mine = jnp.concatenate([h[40:] for h in heads])
    even = jnp.stack([mine] + [swap(mine, "bl", b) for b in range(2, lines, 2)])

    sums = predict(info, heads, comp_position, comp_flux)

    first = swap(sums[1], "comp", 1)
    odd = swap(even, "bl", 1)
    half = sums[0, 1] + first[1]
    second = swap(half, "comp", 2)
    odd, _ = lax.optimization_barrier((odd, half))
    table = jnp.stack([even, odd], 1).reshape(lines, GROUP, 64, per_owner)
    table = table.transpose(2, 0, 1, 3).reshape(64, antennas)

    ready = prepare(info, heads, table)
    res, norm = calibrate(info, heads, ready, (sums[0, 0], first[0], second), antennas)

    res = exchange(list(res))
    norm = lax.all_to_all(norm.reshape(lines * GROUP, per_owner, 96), ("bl", "comp"), 0, 0)
    norm = jnp.sum(norm.reshape(lines, GROUP, per_owner, 24, 4), axis=0)
    normal = norm.transpose(1, 2, 0, 3).reshape(per_owner, 24 * CHANNELS)
    res = jnp.stack(relative(res, core, chip))
    residual = res.reshape(GROUP, 8, 4, rows).transpose(3, 1, 0, 2).reshape(rows, 8 * CHANNELS)
    return (residual, normal)


def solution(mesh):
    rows = P(("bl", "comp"))
    return jax.shard_map(
        local,
        mesh=mesh,
        in_specs=(
            P(None, ("bl", "comp")),
            P(None, ("bl", "comp")),
            rows,
            P(None, "comp"),
            P(None, None, "comp"),
            P(("bl", "comp"), None),
            P(),
            P(("bl", "comp"), None),
        ),
        out_specs=(P(("bl", "comp"), None), P(("bl", "comp"), None)),
        check_vma=False,
    )
```

```python
import jax
import jax.numpy as jnp
from jax import lax
from jax.experimental import pallas as pl
from jax.experimental.pallas import tpu as pltpu
from jax.sharding import PartitionSpec as P

CHANNELS = 16
TIMES = 4
GROUP = 4
LANES = 256
DEPTH = 256
STRIP = 16
F32 = jnp.float32
BF16 = jnp.bfloat16

SIN = [4 * v for v in (4.4428679030304945, -7.307443421264523, 3.5947880783696866, -0.7843740306721513)]
COS = [4 * v for v in (1.4142040804669556, -6.977642056688728, 5.71523839383031, -1.7283486597599615)]
CENTRES = (1 + 3.5 / 32, 1 + 11.5 / 32)
HALF_STEP = 1 / 64
TERMS = ((0, 0), (0, 1), (0, 2), (1, 0), (1, 1), (2, 0))


def pieces(x, count):
    out = []
    for _ in range(count):
        piece = lax.reduce_precision(x, 8, 7)
        out.append(piece.astype(BF16))
        x = x - piece
    return out


def turn(x):
    r = x - jnp.round(x)
    q = r * r
    s = (((SIN[3] * q + SIN[2]) * q + SIN[1]) * q + SIN[0]) * r
    c = ((COS[3] * q + COS[2]) * q + COS[1]) * q + COS[0]
    return 16.0 - s * s, s * c


def factors(t, put):
    for a, centre in enumerate(CENTRES):
        pair = turn(t * centre)
        yield
        for m, v in enumerate(pair):
            hi = jnp.round(v)
            for n, part in enumerate((hi, v - hi, v)):
                put(6 * a + 3 * m + n, part.astype(BF16))
        yield
    c, s = turn(t * HALF_STEP)
    yield
    twice = (c * c) * (4.0 / 256.0) - 2.0
    cs, ss = [c, (twice - 1.0) * c], [s, (twice + 1.0) * s]
    for k in range(4):
        if k > 1:
            cs.append(twice * cs[-1] - cs[-2])
            ss.append(twice * ss[-1] - ss[-2])
        for m, v in enumerate((cs[k], ss[k])):
            hi = jnp.round(v)
            put(12 + 4 * k + 2 * m, hi.astype(BF16))
            put(13 + 4 * k + 2 * m, (v - hi).astype(BF16))
        yield


FACTORS = 28
PIECES = 9


def group_rows(info_ref, heads):
    me = info_ref[0]
    counts = [jnp.max(head[5:6, 0:128]).astype(jnp.int32) for head in heads]
    starts = [
        sum(jnp.where((me ^ c) < (me ^ b), counts[c], 0) for c in range(GROUP)) for b in range(GROUP)
    ]
    return starts, counts, sum(counts)


def place(ref, value, start, count):
    block, off = lax.div(start, LANES), lax.rem(start, LANES)
    lane = lax.broadcasted_iota(jnp.int32, value.shape, 1)
    turned = pltpu.roll(value, off, 1)
    ref[block] = jnp.where((lane >= off) & (lane < off + count), turned, ref[block])
    ref[block + 1] = jnp.where((lane < off) & (lane + LANES < off + count), turned, ref[block + 1])


def taken(ref, start, count):
    block, off = lax.div(start, LANES), lax.rem(start, LANES)
    back = lax.rem(LANES - off, LANES)
    first, second = pltpu.roll(ref[block], back, 1), pltpu.roll(ref[block + 1], back, 1)
    lane = lax.broadcasted_iota(jnp.int32, first.shape, 1)
    return jnp.where(lane < count, jnp.where(lane < LANES - off, first, second), 0.0)


def predict_kernel(blocks, info_ref, h0, h1, h2, h3, l_ref, tab_ref, o_ref, fa, fb, tt, ta, tb, acc, acc2, rows_ref, u_ref):
    starts, counts, live = group_rows(info_ref, (h0, h1, h2, h3))
    half = LANES // 2
    rest_rows = lax.rem(live, LANES)
    halved = (rest_rows > 0) & (rest_rows <= half)
    full = lax.div(live + half - 1, LANES)
    total = full * blocks
    rows_ref[...] = jnp.zeros_like(rows_ref)
    for b, head in enumerate((h0, h1, h2, h3)):
        place(rows_ref, head[0:8], starts[b], counts[b])
    for row in range(u_ref.shape[0]):
        parts, rest = [], rows_ref[row]
        for _ in range(3):
            part = rest.astype(BF16).astype(F32)
            parts.append(part)
            rest = rest - part
        u_ref[row] = jnp.concatenate([parts[i] for i, _ in TERMS], axis=0).astype(BF16)

    def depth(block):
        return pl.ds(pl.multiple_of(block * DEPTH, DEPTH), DEPTH)

    def begin(index, table):
        index = jnp.clip(index, 0, jnp.maximum(total - 1, 0))
        row, block = lax.div(index, blocks), lax.rem(index, blocks)
        tt[...] = jnp.dot(l_ref[depth(block), :], u_ref[row], preferred_element_type=F32)
        table[:, 0:16] = tab_ref[block]

    def begin_halved(index, table):
        index = jnp.minimum(index, blocks // 2 - 1)
        for side in range(2):
            block = 2 * index + side
            tt[:, side * half : side * half + half] = jnp.dot(
                l_ref[depth(block), :], u_ref[full, :, :half], preferred_element_type=F32
            )
            table[:, 16 * side : 16 * side + 16] = tab_ref[block]

    def strips(f):
        for j in range(DEPTH // STRIP):
            rows = slice(j * STRIP, (j + 1) * STRIP)

            def put(i, v, rows=rows):
                f[i, rows] = v

            yield from factors(tt[rows], put)

    def product(d, f, table, into):
        pair, which = d // 4, d % 4
        a, k = pair // 4, pair % 4
        x = 6 * a + (3 if which in (1, 2) else 0)
        y = 12 + 4 * k + (2 if which in (1, 3) else 0)
        t = table[pair, 0 : into.shape[2]]
        hi = f[x] * f[y]
        both = jnp.dot(t, hi, preferred_element_type=F32)
        yield
        lo = f[x + 1] * f[y] + f[x + 2] * f[y + 1]
        both += jnp.dot(t, lo, preferred_element_type=F32)
        yield
        into[pair, which] += both

    def step(f, g, table, into):
        ahead, done, count = strips(g) if g is not None else iter(()), 0, 0
        for d in range(32):
            for _ in product(d, f, table, into):
                count += 1
                while done < count * PIECES * (DEPTH // STRIP) // 64:
                    next(ahead, None)
                    done += 1
        for _ in ahead:
            pass

    def flush(row):
        sign = jnp.where(lax.broadcasted_iota(jnp.int32, (8, LANES), 0) < 4, -1.0, 1.0)
        for pair in range(8):
            a, k = pair // 4, pair % 4
            p = [(acc[pair, w, 0:8] + acc[pair, w, 8:16]) * (1.0 / 256.0) for w in range(4)]
            c = p[0] + sign * p[1]
            s = p[2] - sign * p[3]
            plus, minus = (2 * a + 1) ^ info_ref[0], (2 * a) ^ info_ref[0]
            o_ref[plus & 1, plus >> 1, row, k] = jnp.concatenate([c[0:4], s[0:4]], axis=0)
            o_ref[minus & 1, minus >> 1, row, 3 - k] = jnp.concatenate([c[4:8], s[4:8]], axis=0)
        acc[...] = jnp.zeros_like(acc)

    o_ref[...] = jnp.zeros_like(o_ref)
    acc[...] = jnp.zeros_like(acc)

    def first(start):
        start(0, ta)
        for _ in strips(fa):
            pass

    def twice(start, index, into, count):
        start(index + 1, tb)
        step(fa, fb, ta, into)

        @pl.when(index + 2 < count)
        def _():
            start(index + 2, ta)
            step(fb, fa, tb, into)

        @pl.when(index + 2 >= count)
        def _():
            step(fb, None, tb, into)

    first(begin)

    def body(i, carry):
        twice(begin, 2 * i, acc, total)

        @pl.when(lax.rem(2 * i + 2, blocks) == 0)
        def _():
            flush(lax.div(2 * i, blocks))

        return carry

    lax.fori_loop(0, total // 2, body, 0)

    @pl.when(halved)
    def _():
        acc2[...] = jnp.zeros_like(acc2)
        first(begin_halved)

        def body2(i, carry):
            twice(begin_halved, 2 * i, acc2, blocks // 2)
            return carry

        lax.fori_loop(0, blocks // 4, body2, 0)
        for pair in range(8):
            for w in range(4):
                z = acc2[pair, w, 0:16, :half] + acc2[pair, w, 16:32, half:]
                acc[pair, w] = jnp.concatenate([z, jnp.zeros_like(z)], axis=1)
        flush(full)


def predict(info, heads, position, flux):
    comps = position.shape[1]
    row_blocks, blocks = GROUP, comps // DEPTH
    l_coord, m_coord = position[0], position[1]
    n_minus = jnp.sqrt(1.0 - l_coord * l_coord - m_coord * m_coord) - 1.0
    lp = pieces(jnp.pad(jnp.stack([l_coord, m_coord, n_minus]), ((0, 5), (0, 0))), 3)
    l = jnp.concatenate([lp[j] for _, j in TERMS]).T
    i, q, v, w = flux
    bright = jnp.stack([i + q, v, w, i - q], 1).reshape(2, 8, 4, comps)
    plus, minus = bright[:, 4:].reshape(8, 4, comps), bright[:, 3::-1].reshape(8, 4, comps)
    hi, lo = pieces(jnp.concatenate([plus, minus], 1), 2)
    table = jnp.concatenate([hi, lo], 1).reshape(8, 16, blocks, DEPTH).transpose(2, 0, 1, 3)
    vmem = pl.BlockSpec(memory_space=pltpu.VMEM)
    return pl.pallas_call(
        lambda *refs: predict_kernel(blocks, *refs),
        out_shape=jax.ShapeDtypeStruct((2, 2, row_blocks, 4, 8, LANES), F32),
        in_specs=[pl.BlockSpec(memory_space=pltpu.SMEM)] + [vmem] * 6,
        out_specs=vmem,
        scratch_shapes=[
            pltpu.VMEM((FACTORS, DEPTH, LANES), BF16),
            pltpu.VMEM((FACTORS, DEPTH, LANES), BF16),
            pltpu.VMEM((DEPTH, LANES), F32),
            pltpu.VMEM((8, 32, DEPTH), BF16),
            pltpu.VMEM((8, 32, DEPTH), BF16),
            pltpu.VMEM((8, 4, 16, LANES), F32),
            pltpu.VMEM((8, 4, 32, LANES), F32),
            pltpu.VMEM((row_blocks + 1, 8, LANES), F32),
            pltpu.VMEM((row_blocks, 48, LANES), BF16),
        ],
        compiler_params=pltpu.CompilerParams(vmem_limit_bytes=40 << 20),
        cost_estimate=pl.CostEstimate(
            flops=64 * 16 * GROUP * LANES * comps, bytes_accessed=4 << 20, transcendentals=0
        ),
        name="predict",
    )(info, *heads, l, table)


def prepare_kernel(info_ref, h0, h1, h2, h3, table_ref, obs_ref, slot_ref, picked_ref, gain_ref):
    slots = table_ref.shape[1]
    flip = info_ref[1]
    starts, counts, live = group_rows(info_ref, (h0, h1, h2, h3))
    obs_ref[...] = jnp.zeros_like(obs_ref)
    slot_ref[...] = jnp.zeros_like(slot_ref)
    for b, head in enumerate((h0, h1, h2, h3)):
        place(slot_ref, head[0:8], starts[b], counts[b])
        place(obs_ref, head[8:40], starts[b], counts[b])
    rest = table_ref[...]
    for p in range(3):
        part = rest.astype(BF16)
        gain_ref[64 * p : 64 * p + 64] = part
        rest = rest - part.astype(F32)

    def block(row, carry):
        lane = lax.broadcasted_iota(jnp.int32, (1, LANES), 1)
        time = [(lax.rem(lane, TIMES) == t).astype(F32) for t in range(TIMES)]
        slot = lax.broadcasted_iota(jnp.int32, (slots, LANES), 0)
        for end in range(2):
            at = slot_ref[row, 3 + end : 4 + end].astype(jnp.int32)
            hot = jnp.where(slot == (at ^ flip), 1.0, 0.0).astype(BF16)
            g = jnp.dot(gain_ref[...], hot, preferred_element_type=F32)
            g = g[0:64] + g[64:128] + g[128:192]
            picked_ref[row, end] = sum(g[16 * t : 16 * t + 16] * time[t] for t in range(TIMES))
        return carry

    lax.fori_loop(0, lax.div(live + LANES - 1, LANES), block, 0)


def calibrate_kernel(info_ref, h0, h1, h2, h3, obs_ref, slot_ref, picked_ref, own_ref, near_ref, far_ref, out_ref, sum_ref, res_ref, norm_ref):
    slots = norm_ref.shape[0]
    starts, counts, live = group_rows(info_ref, (h0, h1, h2, h3))
    norm_ref[...] = jnp.zeros_like(norm_ref)
    res_ref[...] = jnp.zeros_like(res_ref)

    def block(row, carry):
        lane = lax.broadcasted_iota(jnp.int32, (1, LANES), 1)
        weight = (lane + row * LANES < live).astype(F32)
        time = [(lax.rem(lane, TIMES) == t).astype(F32) for t in range(TIMES)]
        slot = lax.broadcasted_iota(jnp.int32, (slots, LANES), 0)
        hots, gains = [], []
        for end in range(2):
            at = slot_ref[row, 3 + end : 4 + end].astype(jnp.int32)
            hots.append(jnp.where(slot == at, 1.0, 0.0).astype(BF16))
            picked = picked_ref[row, end]
            gains.append([[picked[8 * part + 4 * pol : 8 * part + 4 * pol + 4] for pol in range(2)] for part in range(2)])
        sums = own_ref[row] + near_ref[row] + far_ref[row]
        c = [sums[:, n] for n in range(4)]
        s = [sums[:, 4 + n] for n in range(4)]
        vis_r = [[c[0], c[1] + s[2]], [c[1] - s[2], c[3]]]
        vis_i = [[-s[0], c[2] - s[1]], [-c[2] - s[1], -s[3]]]
        (near_r, near_i), (far_r, far_i) = gains
        near = [[0.0, 0.0], [0.0, 0.0], [0.0, 0.0]]
        far = [[0.0, 0.0], [0.0, 0.0], [0.0, 0.0]]
        for a in range(2):
            for b in range(2):
                vr, vi = vis_r[a][b], vis_i[a][b]
                zr = far_r[b] * vr + far_i[b] * vi
                zi = far_r[b] * vi - far_i[b] * vr
                yr = near_r[a] * vr - near_i[a] * vi
                yi = near_r[a] * vi + near_i[a] * vr
                mr = near_r[a] * zr - near_i[a] * zi
                mi = near_r[a] * zi + near_i[a] * zr
                at = (a * 2 + b) * 4
                rr = weight * (obs_ref[row, at : at + 4] - mr)
                ri = weight * (obs_ref[row, 16 + at : 16 + at + 4] - mi)
                res_ref[row, at : at + 4] = rr
                res_ref[row, 16 + at : 16 + at + 4] = ri
                near[0][a] += weight * (zr * zr + zi * zi)
                near[1][a] += zr * rr + zi * ri
                near[2][a] += zr * ri - zi * rr
                far[0][b] += weight * (yr * yr + yi * yi)
                far[1][b] += yr * rr + yi * ri
                far[2][b] += yi * rr - yr * ri
        terms = []
        for end in (near, far):
            flat = jnp.concatenate([end[k][pol] for k in range(3) for pol in range(2)], axis=0)
            whole = jnp.concatenate([flat * time[t] for t in range(TIMES)], axis=0)
            hi = whole.astype(BF16)
            lo = (whole - hi.astype(F32)).astype(BF16)
            terms.append(jnp.concatenate([hi, lo], axis=0))
        both = lax.dot_general(
            jnp.concatenate(hots, axis=1),
            jnp.concatenate(terms, axis=1),
            (((1,), (1,)), ((), ())),
            preferred_element_type=F32,
        )
        norm_ref[...] += both
        return carry

    lax.fori_loop(0, lax.div(live + LANES - 1, LANES), block, 0)
    sum_ref[...] = norm_ref[:, :96] + norm_ref[:, 96:]
    for b in range(GROUP):
        out_ref[b] = taken(res_ref, starts[b], counts[b])


VMEM = pl.BlockSpec(memory_space=pltpu.VMEM)
SMEM = pl.BlockSpec(memory_space=pltpu.SMEM)


def prepare(info, heads, table):
    return pl.pallas_call(
        prepare_kernel,
        out_shape=(
            jax.ShapeDtypeStruct((GROUP + 1, 32, LANES), F32),
            jax.ShapeDtypeStruct((GROUP + 1, 8, LANES), F32),
            jax.ShapeDtypeStruct((GROUP, 2, 16, LANES), F32),
        ),
        in_specs=[SMEM] + [VMEM] * 5,
        out_specs=(VMEM, VMEM, VMEM),
        scratch_shapes=[pltpu.VMEM((192, table.shape[1]), BF16)],
        compiler_params=pltpu.CompilerParams(vmem_limit_bytes=16 << 20),
        cost_estimate=pl.CostEstimate(flops=1 << 30, bytes_accessed=1 << 20, transcendentals=0),
        name="prepare",
    )(info, *heads, table)


def calibrate(info, heads, ready, parts, antennas):
    return pl.pallas_call(
        calibrate_kernel,
        out_shape=(
            jax.ShapeDtypeStruct((GROUP, 32, LANES), F32),
            jax.ShapeDtypeStruct((antennas, 96), F32),
        ),
        in_specs=[SMEM] + [VMEM] * 10,
        out_specs=(VMEM, VMEM),
        scratch_shapes=[
            pltpu.VMEM((GROUP + 1, 32, LANES), F32),
            pltpu.VMEM((antennas, 192), F32),
        ],
        compiler_params=pltpu.CompilerParams(vmem_limit_bytes=24 << 20),
        name="calibrate",
    )(info, *heads, *ready, *parts)


def swap(value, axis, bits):
    count = lax.axis_size(axis)
    return lax.ppermute(value, axis, [(d, d ^ bits) for d in range(count)])


def relative(values, core, chip):
    values = [jnp.where(core, values[j ^ 1], values[j]) for j in range(GROUP)]
    return [jnp.where(chip, values[j ^ 2], values[j]) for j in range(GROUP)]


def exchange(values):
    return [values[0]] + [swap(values[b], "comp", b) for b in range(1, GROUP)]


def owner_slots(antenna_owner, per_owner):
    index = jnp.arange(antenna_owner.shape[0], dtype=jnp.int32)
    same = (antenna_owner[None, :] == antenna_owner[:, None]) & (index[None, :] < index[:, None])
    return antenna_owner * per_owner + jnp.sum(same.astype(jnp.int32), axis=1)


def row_slots(antennas, slots):
    index = jnp.arange(slots.shape[0], dtype=jnp.int32)
    return jnp.sum(jnp.where(antennas[..., None] == index, slots, 0), axis=-1)


def local(baseline_uvw, antenna_pair, row_count, comp_position, comp_flux, gain, antenna_owner, observed):
    rows = baseline_uvw.shape[1]
    antennas = antenna_owner.shape[0]
    lines = lax.axis_size("bl")
    per_owner = antennas // (lines * GROUP)
    me_comp, me_line = lax.axis_index("comp"), lax.axis_index("bl")
    core, chip = (me_comp & 1) != 0, me_comp >= 2

    slots = row_slots(antenna_pair, owner_slots(antenna_owner, per_owner))
    count = jnp.broadcast_to(row_count[:, None], (3, rows))
    head = jnp.concatenate([baseline_uvw, slots.astype(F32), count.astype(F32)])
    part = gain.reshape(per_owner, 16, GROUP, 4).transpose(2, 1, 3, 0).reshape(GROUP, -1, rows)
    part = relative(list(part), core, chip)
    obs = observed.reshape(rows, 8, GROUP, 4).transpose(2, 1, 3, 0).reshape(GROUP, 32, rows)
    obs = relative(list(obs), core, chip)
    heads = exchange([jnp.concatenate([head, o, p]) for o, p in zip(obs, part)])
    info = jnp.stack([me_comp, (me_line * GROUP + me_comp) * per_owner]).astype(jnp.int32)

    mine = jnp.concatenate([h[40:] for h in heads])
    even = jnp.stack([mine] + [swap(mine, "bl", b) for b in range(2, lines, 2)])

    sums = predict(info, heads, comp_position, comp_flux)

    first = swap(sums[1], "comp", 1)
    odd = swap(even, "bl", 1)
    half = sums[0, 1] + first[1]
    second = swap(half, "comp", 2)
    odd, _ = lax.optimization_barrier((odd, half))
    table = jnp.stack([even, odd], 1).reshape(lines, GROUP, 64, per_owner)
    table = table.transpose(2, 0, 1, 3).reshape(64, antennas)

    ready = prepare(info, heads, table)
    res, norm = calibrate(info, heads, ready, (sums[0, 0], first[0], second), antennas)

    res = exchange(list(res))
    norm = lax.all_to_all(norm.reshape(lines * GROUP, per_owner, 96), ("bl", "comp"), 0, 0)
    norm = jnp.sum(norm.reshape(lines, GROUP, per_owner, 24, 4), axis=0)
    normal = norm.transpose(1, 2, 0, 3).reshape(per_owner, 24 * CHANNELS)
    res = jnp.stack(relative(res, core, chip))
    residual = res.reshape(GROUP, 8, 4, rows).transpose(3, 1, 0, 2).reshape(rows, 8 * CHANNELS)
    return (residual, normal)


def solution(mesh):
    rows = P(("bl", "comp"))
    return jax.shard_map(
        local,
        mesh=mesh,
        in_specs=(
            P(None, ("bl", "comp")),
            P(None, ("bl", "comp")),
            rows,
            P(None, "comp"),
            P(None, None, "comp"),
            P(("bl", "comp"), None),
            P(),
            P(("bl", "comp"), None),
        ),
        out_specs=(P(("bl", "comp"), None), P(("bl", "comp"), None)),
        check_vma=False,
    )
```
